32 devices in a mesh: group: 2 (over y), wide: 4 (over z), sub: 2 (over x), pol: 2 (over core).
Axes of the slice: x: 2, y: 2, z: 4, core: 2. Of those that a mesh axis runs over, the one named last changes fastest.
Arguments:
- voltages: bfloat16 [2, 2048, 4, 2048], P('pol', ('group', 'wide'), 'sub'), parts along dimension 1, may hold values from -6 to 6
- real_weight: bfloat16 [512, 1024, 256], P(('wide', 'sub', 'pol')), may hold values from -0.125 to 0.125
- imaginary_weight: bfloat16 [512, 1024, 256], P(('wide', 'sub', 'pol')), may hold values from -0.125 to 0.125
- delays: int32 [128, 512], P('pol'), may hold values from 0 to 3
Outputs:
- dedispersed: float32 [512, 4, 128], P(('group', 'wide', 'sub'), None, 'pol'), parts along dimension 0
The draws below stay inside these ranges and needn't reach their ends.
There are 2 independent parts, one for each index of `group`. The reference program is written for one: setup_inputs(seed, part) draws one part's arguments, and reference() takes and returns one part's arrays. A program takes and returns all parts, laid end to end along the dimension named above; an argument that names none is the same for every part. Nothing has to cross between parts.
Inputs may be any that keep to these rules, and one draw needn't show every extreme that they name: `delays`: integer sample shifts of each delay trial and channel.
All inputs are finite; a program needn't handle non-finite values.
Results may differ from the reference program's by a relative error of at most 0.012.
Values may be sent and summed in bfloat16 or wider, within the bound.
No kernel may reach another device: no remote copies, remote signals or barrier semaphores. Data moves between devices by JAX's collectives and lax.ppermute only.
A program may use at most 256 MiB of HBM per device.

```python
import math
import jax
import jax.numpy as jnp
from jax import lax

ANTENNA_COUNT = 1024
FRAME_SAMPLES = 2048
CHANNEL_COUNT = 512
BEAM_COUNT = 256
TRIALS = 128
FRAME_COUNT = 4


def plant(values, stream_key, least, largest):
    longest = values.shape.index(max(values.shape))
    spots = []
    for shift in (0, 1):
        where = [jax.random.randint(jax.random.fold_in(stream_key, axis), (), 0, length) for axis, length in enumerate(values.shape)]
        where[longest] = (where[longest] + shift) % values.shape[longest]
        spots.append(tuple(where))
    return values.at[spots[0]].set(least).at[spots[1]].set(largest)


def shard_levels(own_key, shape, split, low, largest):
    level = 1.0
    for dim, blocks in split:
        heights = jax.random.uniform(jax.random.fold_in(jax.random.fold_in(own_key, 6), dim), (blocks,), jnp.float32, low / len(split), largest / len(split))
        level = level * jnp.repeat(jnp.exp(heights), shape[dim] // blocks).reshape((-1,) + (1,) * (len(shape) - 1 - dim))
    return level


def normal_values(rng, dims, width, bound, split=(), dtype=jnp.bfloat16):
    values = width * jax.random.normal(rng, dims, jnp.float32)
    if split:
        values = values * shard_levels(rng, dims, split, -0.22, 0.18)
    return jnp.clip(values, -bound, bound).astype(dtype)


def setup_inputs(seed: int = 0, part: int = 0) -> dict:
    seeds = jax.random.split(jax.random.key(seed), 5)
    part_keys = jax.random.split(jax.random.fold_in(seeds[4], part), 5)
    return {
        "voltages": normal_values(part_keys[0], (2, ANTENNA_COUNT, FRAME_COUNT, FRAME_SAMPLES), 1.0, 6.0, ((0, 2), (1, 4), (2, 2))),
        "real_weight": normal_values(seeds[1], (CHANNEL_COUNT, ANTENNA_COUNT, BEAM_COUNT), (2 * ANTENNA_COUNT) ** -0.5, 0.125, ((0, 16),)),
        "imaginary_weight": normal_values(seeds[2], (CHANNEL_COUNT, ANTENNA_COUNT, BEAM_COUNT), (2 * ANTENNA_COUNT) ** -0.5, 0.125, ((0, 16),)),
        "delays": plant(jax.random.randint(seeds[3], (TRIALS, CHANNEL_COUNT), 0, FRAME_COUNT), jax.random.fold_in(seeds[3], 1), 0, FRAME_COUNT - 1).astype(jnp.int32),
    }


def reference(voltages, real_weight, imaginary_weight, delays):
    first_bin = FRAME_SAMPLES // 2 - CHANNEL_COUNT
    spectrum = jnp.fft.rfft(voltages.astype(jnp.float32), axis=-1)[..., first_bin:first_bin + CHANNEL_COUNT] / math.sqrt(FRAME_SAMPLES)
    x_re = jnp.real(spectrum).astype(jnp.bfloat16)
    x_im = jnp.imag(spectrum).astype(jnp.bfloat16)
    input_arrays = jnp.concatenate([x_re, x_im], axis=1)
    input_arrays = jnp.transpose(input_arrays, (3, 0, 2, 1)).reshape(CHANNEL_COUNT, 2 * FRAME_COUNT, 2 * ANTENNA_COUNT)
    channel_block = math.gcd(CHANNEL_COUNT, 16)

    def beam_tile(triple):
        left, real_part, imag_part = triple
        upper = jnp.concatenate([real_part, imag_part], axis=2)
        lower = jnp.concatenate([-imag_part, real_part], axis=2)
        real_form = jnp.concatenate([upper, lower], axis=1)
        return jnp.einsum('cra,cab->crb', left.astype(jnp.float32), real_form.astype(jnp.float32), precision=lax.Precision.HIGHEST)
    beam_output = lax.map(beam_tile, (input_arrays.reshape(-1, channel_block, 2 * FRAME_COUNT, 2 * ANTENNA_COUNT), real_weight.reshape(-1, channel_block, ANTENNA_COUNT, BEAM_COUNT), imaginary_weight.reshape(-1, channel_block, ANTENNA_COUNT, BEAM_COUNT)))
    beam_field = beam_output.reshape(CHANNEL_COUNT, 2, FRAME_COUNT, 2, BEAM_COUNT)
    power = lax.optimization_barrier(jnp.sum(beam_field * beam_field, axis=(1, 3)))
    centered = power - lax.optimization_barrier(jnp.mean(power, axis=1, keepdims=True))
    frame_ids = jnp.arange(FRAME_COUNT).astype(jnp.int32)

    def one_trial(delay_row):
        index = (frame_ids[None, :] + delay_row[:, None].astype(jnp.int32)) % FRAME_COUNT
        index = jnp.broadcast_to(index[:, :, None], centered.shape)
        return lax.optimization_barrier(jnp.sum(jnp.take_along_axis(centered, index, axis=1), axis=0))
    result = lax.map(one_trial, delays)
    return jnp.transpose(result, (2, 1, 0)) / math.sqrt(CHANNEL_COUNT)
```

```python
import functools
import math

import jax
import jax.numpy as jnp
import ml_dtypes
import numpy as np
from jax import lax
from jax.experimental import pallas as pl
from jax.experimental.pallas import tpu as pltpu
from jax.sharding import PartitionSpec as P

OWNERS = ("wide", "sub", "pol")
ROWS = 16


def dft_parts(samples, channels):
    first = samples // 2 - channels
    bins = first + np.arange(channels, dtype=np.int64)
    turns = bins[:, None] * np.arange(samples, dtype=np.int64)[None, :] % samples
    angles = turns * (2.0 * math.pi / samples)
    exact = np.stack([np.cos(angles), -np.sin(angles)], axis=1) / math.sqrt(samples)
    upper = exact.astype(ml_dtypes.bfloat16)
    lower = (exact - upper.astype(np.float64)).astype(ml_dtypes.bfloat16)
    return upper, lower


def dft_kernel(table_ref, volt_ref, out_ref):
    rows = out_ref.shape[0] * out_ref.shape[2]
    for frame in range(volt_ref.shape[0]):
        both = lax.dot_general(
            table_ref[0],
            volt_ref[frame],
            (((1,), (1,)), ((), ())),
            preferred_element_type=jnp.float32,
        )
        spectrum = (both[:rows] + both[rows:]).astype(jnp.bfloat16)
        out_ref[:, frame] = spectrum.reshape(out_ref.shape[0], out_ref.shape[2], -1)


def spectra(volts, owners, channels):
    frames, antennas, samples = volts.shape
    own = channels // owners
    upper, lower = dft_parts(samples, channels)
    group = ROWS // 2

    def order(part):
        part = part.reshape(owners, own // group, group, 2, samples)
        return part.transpose(0, 1, 3, 2, 4).reshape(owners, 2 * own, samples)

    upper, lower = order(upper), order(lower)
    step = max(1, min(owners, 256 // (2 * own)))
    while owners % step:
        step -= 1
    steps = owners // step
    table = np.concatenate(
        [
            upper.reshape(steps, step * 2 * own, samples),
            lower.reshape(steps, step * 2 * own, samples),
        ],
        axis=1,
    )
    return pl.pallas_call(
        dft_kernel,
        grid=(steps,),
        in_specs=[
            pl.BlockSpec((1,) + table.shape[1:], lambda i: (i, 0, 0)),
            pl.BlockSpec(volts.shape, lambda i: (0, 0, 0)),
        ],
        out_specs=pl.BlockSpec((step, frames, 2 * own, antennas), lambda i: (i, 0, 0, 0)),
        out_shape=jax.ShapeDtypeStruct((owners, frames, 2 * own, antennas), jnp.bfloat16),
        compiler_params=pltpu.CompilerParams(vmem_limit_bytes=48 * 2**20),
        name="spectra",
    )(jnp.asarray(table), volts)


def beam_kernel(sources, wides, order_ref, x_ref, re_ref, im_ref, out_ref, sorted_ref, power_ref):
    group = re_ref.shape[0]
    per_wide = sources // wides
    frames = x_ref.shape[1]
    for wide in range(wides):
        block = x_ref[pl.ds(wide * per_wide, per_wide)]
        block = block.reshape(per_wide * frames * ROWS, block.shape[-1])
        ordered = jnp.dot(order_ref[...], block, preferred_element_type=jnp.float32)
        sorted_ref[:, wide * block.shape[-1] : (wide + 1) * block.shape[-1]] = ordered.astype(
            jnp.bfloat16
        )
    half = per_wide * frames
    total = half // 2
    for channel in range(group):
        rows = sorted_ref[channel * 2 * half : (channel + 1) * 2 * half, :]
        by_re = jnp.dot(rows, re_ref[channel], preferred_element_type=jnp.float32)
        by_im = jnp.dot(rows, im_ref[channel], preferred_element_type=jnp.float32)
        beam_re = by_re[:half] - by_im[half:]
        beam_im = by_im[:half] + by_re[half:]
        power = beam_re * beam_re + beam_im * beam_im
        power = power[:total] + power[total:]
        power = power - jnp.mean(power, axis=0, keepdims=True)
        power_ref[:, channel, :] = power
    targets = out_ref.shape[0]
    beams = power_ref.shape[2] // targets
    for target in range(targets):
        block = jnp.concatenate(
            [power_ref[f, :, target * beams : (target + 1) * beams] for f in range(total)], axis=1
        )
        out_ref[target] = block.astype(jnp.bfloat16)


def beam_power(x, real_weight, imaginary_weight, wides, subs, pols):
    sources, frames, _, antennas = x.shape
    channels, antenna_total, beams = real_weight.shape
    group = ROWS // 2
    per_wide = sources // wides
    count = per_wide * frames * ROWS
    place = np.arange(count).reshape(subs, pols, frames, 2, group).transpose(4, 3, 1, 0, 2).reshape(-1)
    order = np.zeros((count, count), np.float32)
    order[np.arange(count), place] = 1.0
    targets = wides * subs
    width = subs * frames * (beams // targets)
    return pl.pallas_call(
        functools.partial(beam_kernel, sources, wides),
        grid=(channels // group,),
        in_specs=[
            pl.BlockSpec((count, count), lambda i: (0, 0)),
            pl.BlockSpec((sources, frames, ROWS, antennas), lambda i: (0, 0, i, 0)),
            pl.BlockSpec((group, antenna_total, beams), lambda i: (i, 0, 0)),
            pl.BlockSpec((group, antenna_total, beams), lambda i: (i, 0, 0)),
        ],
        out_specs=pl.BlockSpec((targets, group, width), lambda i: (0, i, 0)),
        out_shape=jax.ShapeDtypeStruct((targets, channels, width), jnp.bfloat16),
        scratch_shapes=[
            pltpu.VMEM((count, antenna_total), jnp.bfloat16),
            pltpu.VMEM((subs * frames, group, beams), jnp.float32),
        ],
        compiler_params=pltpu.CompilerParams(vmem_limit_bytes=48 * 2**20),
        name="beam_power",
    )(jnp.asarray(order, jnp.bfloat16), x, real_weight, imaginary_weight)


def shift_kernel(scale, power_ref, delay_ref, out_ref):
    beams, frames, _ = out_ref.shape
    delays = delay_ref[...]
    power = power_ref[...]
    sums = [None] * frames
    for delay in range(frames):
        chosen = (delays == delay).astype(jnp.float32).astype(jnp.bfloat16)
        picked = lax.dot_general(
            power, chosen, (((0,), (1,)), ((), ())), preferred_element_type=jnp.float32
        )
        for frame in range(frames):
            row = (frame + delay) % frames * beams
            term = picked[row : row + beams]
            sums[frame] = term if sums[frame] is None else sums[frame] + term
    for frame in range(frames):
        out_ref[:, frame, :] = sums[frame] * scale


def shift_and_add(power, delays, frames):
    channels, width = power.shape
    beams = width // frames
    return pl.pallas_call(
        functools.partial(shift_kernel, 1.0 / math.sqrt(channels)),
        out_shape=jax.ShapeDtypeStruct((beams, frames, delays.shape[0]), jnp.float32),
        name="shift_and_add",
    )(power, delays % frames)


def plain_spectra(volts, owners, channels):
    frames, antennas, samples = volts.shape
    upper, lower = (jnp.asarray(part) for part in dft_parts(samples, channels))
    x = sum(
        jnp.einsum("krn,fan->kfra", part, volts, preferred_element_type=jnp.float32)
        for part in (upper, lower)
    )
    x = x.astype(jnp.bfloat16).reshape(owners, channels // owners, frames, 2, antennas)
    return x


def plain_beam_power(x, real_weight, imaginary_weight, wides, subs, pols):
    _, own, frames, _, antennas = x.shape
    beams = real_weight.shape[2]
    x = x.reshape(wides, subs, pols, own, frames, 2, antennas)
    x = x.transpose(3, 5, 2, 1, 4, 0, 6).reshape(own, 2, pols * subs * frames, wides * antennas)
    by_re, by_im = (
        jnp.einsum("crfa,cab->rcfb", x, weight, preferred_element_type=jnp.float32)
        for weight in (real_weight, imaginary_weight)
    )
    power = (by_re[0] - by_im[1]) ** 2 + (by_im[0] + by_re[1]) ** 2
    power = power.reshape(own, pols, subs * frames, beams).sum(axis=1)
    power = power - jnp.mean(power, axis=1, keepdims=True)
    targets = wides * subs
    power = power.reshape(own, subs * frames, targets, beams // targets)
    return power.transpose(2, 0, 1, 3).reshape(targets, own, -1).astype(jnp.bfloat16)


def plain_shift_and_add(power, delays, frames):
    channels = power.shape[0]
    power = power.reshape(channels, frames, -1)
    chosen = (delays[None] % frames == jnp.arange(frames)[:, None, None]).astype(jnp.bfloat16)
    picked = jnp.einsum("dtc,cfb->dbft", chosen, power, preferred_element_type=jnp.float32)
    moved = sum(jnp.roll(picked[delay], -delay, axis=1) for delay in range(frames))
    return moved * (1.0 / math.sqrt(channels))


def local(voltages, real_weight, imaginary_weight, delays):
    wides, subs, pols = (lax.axis_size(name) for name in OWNERS)
    owners = wides * subs * pols
    own, _, beams = real_weight.shape
    frames = subs * voltages.shape[2]
    volts = jnp.transpose(voltages[0], (1, 0, 2))
    tiled = (
        own % ROWS == 0
        and voltages.shape[1] % 128 == 0
        and (beams // (wides * subs)) % 32 == 0
        and frames == 4
        and pols == 2
    )
    form = spectra if tiled else plain_spectra
    beamform = beam_power if tiled else plain_beam_power
    finish = shift_and_add if tiled else plain_shift_and_add
    x = form(volts, owners, own * owners)
    x = lax.all_to_all(x, OWNERS, split_axis=0, concat_axis=0, tiled=True)
    power = beamform(x, real_weight, imaginary_weight, wides, subs, pols)
    width = power.shape[2]
    power = jnp.broadcast_to(power[:, None], (wides * subs, pols, own, width))
    power = power.reshape(owners, own, width)
    power = lax.all_to_all(power, OWNERS, split_axis=0, concat_axis=0, tiled=True)
    return finish(power.reshape(owners * own, width), delays, frames)


def solution(mesh):
    placed = (
        P("pol", ("group", "wide"), "sub", None),
        P(OWNERS, None, None),
        P(OWNERS, None, None),
        P("pol", None),
    )
    return jax.shard_map(
        local,
        mesh=mesh,
        in_specs=placed,
        out_specs=P(("group", "wide", "sub"), None, "pol"),
        check_vma=False,
    )
```

```python
import functools
import math

import jax
import jax.numpy as jnp
import ml_dtypes
import numpy as np
from jax import lax
from jax.experimental import pallas as pl
from jax.experimental.pallas import tpu as pltpu
from jax.sharding import PartitionSpec as P

OWNERS = ("wide", "sub", "pol")
ROWS = 16


def dft_parts(samples, channels):
    first = samples // 2 - channels
    bins = first + np.arange(channels, dtype=np.int64)
    turns = bins[:, None] * np.arange(samples, dtype=np.int64)[None, :] % samples
    angles = turns * (2.0 * math.pi / samples)
    exact = np.stack([np.cos(angles), -np.sin(angles)], axis=1) / math.sqrt(samples)
    upper = exact.astype(ml_dtypes.bfloat16)
    lower = (exact - upper.astype(np.float64)).astype(ml_dtypes.bfloat16)
    return upper, lower


def dft_kernel(table_ref, volt_ref, out_ref, part_ref, sem):
    steps, rows = part_ref.shape[:2]
    frames = volt_ref.shape[0]
    owners = out_ref.shape[0] // steps
    copies = [
        pltpu.make_async_copy(table_ref.at[step], part_ref.at[step], sem.at[step])
        for step in range(steps)
    ]
    for copy in copies:
        copy.start()
    for step, copy in enumerate(copies):
        copy.wait()
        for frame in range(frames):
            both = lax.dot_general(
                part_ref[step],
                volt_ref[frame],
                (((1,), (1,)), ((), ())),
                preferred_element_type=jnp.float32,
            )
            spectrum = (both[: rows // 2] + both[rows // 2 :]).astype(jnp.bfloat16)
            out_ref[step * owners : (step + 1) * owners, frame] = spectrum.reshape(
                owners, -1, spectrum.shape[-1]
            )


def spectra(volts, owners, channels):
    frames, antennas, samples = volts.shape
    own = channels // owners
    group = ROWS // 2
    step = max(1, min(owners, 256 // (2 * own)))
    while owners % step:
        step -= 1
    steps = owners // step

    def order(part):
        part = part.reshape(steps, step, own // group, group, 2, samples)
        return part.transpose(0, 1, 2, 4, 3, 5).reshape(steps, -1, samples)

    table = np.concatenate([order(part) for part in dft_parts(samples, channels)], axis=1)
    vmem = pl.BlockSpec(memory_space=pltpu.VMEM)
    return pl.pallas_call(
        dft_kernel,
        in_specs=[pl.BlockSpec(memory_space=pltpu.HBM), vmem],
        out_specs=vmem,
        out_shape=jax.ShapeDtypeStruct((owners, frames, 2 * own, antennas), jnp.bfloat16),
        scratch_shapes=[
            pltpu.VMEM(table.shape, jnp.bfloat16),
            pltpu.SemaphoreType.DMA((steps,)),
        ],
        compiler_params=pltpu.CompilerParams(vmem_limit_bytes=14 * 2**20),
        name="spectra",
    )(
        pltpu.with_memory_space_constraint(jnp.asarray(table), pltpu.HBM),
        pltpu.with_memory_space_constraint(volts, pltpu.VMEM),
    )


def beam_kernel(wides, order_ref, x_ref, re_ref, im_ref, out_ref, held_ref, sorted_ref, power_ref, sem):
    sources, frames, rows, antennas = x_ref.shape
    per_wide = sources // wides
    half = per_wide * frames
    total = half // 2
    group = ROWS // 2

    def fetch(own):
        return pltpu.make_async_copy(im_ref.at[own], held_ref.at[own], sem.at[own])

    for own in range(rows // 2):
        fetch(own).start()

    def one_group(step, carry):
        start = pl.multiple_of(step * ROWS, ROWS)
        for wide in range(wides):
            block = x_ref[pl.ds(wide * per_wide, per_wide), :, pl.ds(start, ROWS), :]
            block = block.reshape(half * ROWS, antennas)
            ordered = jnp.dot(order_ref[...], block, preferred_element_type=jnp.float32)
            sorted_ref[:, wide * antennas : (wide + 1) * antennas] = ordered.astype(jnp.bfloat16)
        for channel in range(group):
            fetch(step * group + channel).wait()
        for channel in range(group):
            own = step * group + channel
            lines = sorted_ref[channel * 2 * half : (channel + 1) * 2 * half, :]
            by_re = jnp.dot(lines, re_ref[own], preferred_element_type=jnp.float32)
            by_im = jnp.dot(lines, held_ref[own], preferred_element_type=jnp.float32)
            beam_re = by_re[:half] - by_im[half:]
            beam_im = by_im[:half] + by_re[half:]
            power = beam_re * beam_re + beam_im * beam_im
            power = power[:total] + power[total:]
            power = power - jnp.mean(power, axis=0, keepdims=True)
            power_ref[step, :, channel, :] = power
        return carry

    steps = rows // ROWS
    lax.fori_loop(0, steps, one_group, 0)
    targets, copies = out_ref.shape[:2]
    beams = power_ref.shape[3] // targets
    for target in range(targets):
        block = jnp.concatenate(
            [
                power_ref[:, f, :, target * beams : (target + 1) * beams].reshape(-1, beams)
                for f in range(total)
            ],
            axis=1,
        ).astype(jnp.bfloat16)
        for copy in range(copies):
            out_ref[target, copy] = block


def beam_power(x, real_weight, imaginary_weight, wides, subs, pols):
    sources, frames, _, _ = x.shape
    channels, antenna_total, beams = real_weight.shape
    group = ROWS // 2
    half = sources // wides * frames
    count = half * ROWS
    place = np.arange(count).reshape(subs, pols, frames, 2, group).transpose(4, 3, 1, 0, 2).reshape(-1)
    order = np.zeros((count, count), np.float32)
    order[np.arange(count), place] = 1.0
    targets = wides * subs
    width = subs * frames * (beams // targets)
    vmem = pl.BlockSpec(memory_space=pltpu.VMEM)
    return pl.pallas_call(
        functools.partial(beam_kernel, wides),
        in_specs=[vmem] * 3 + [pl.BlockSpec(memory_space=pltpu.HBM)],
        out_specs=vmem,
        out_shape=jax.ShapeDtypeStruct((targets, pols, channels, width), jnp.bfloat16),
        scratch_shapes=[
            pltpu.VMEM(imaginary_weight.shape, jnp.bfloat16),
            pltpu.VMEM((count, antenna_total), jnp.bfloat16),
            pltpu.VMEM((channels // group, subs * frames, group, beams), jnp.float32),
            pltpu.SemaphoreType.DMA((channels,)),
        ],
        compiler_params=pltpu.CompilerParams(vmem_limit_bytes=24 * 2**20),
        name="beam_power",
    )(
        jnp.asarray(order, jnp.bfloat16),
        x,
        pltpu.with_memory_space_constraint(real_weight, pltpu.VMEM),
        pltpu.with_memory_space_constraint(imaginary_weight, pltpu.HBM),
    )


def shift_kernel(scale, power_ref, delay_ref, out_ref):
    beams, frames, _ = out_ref.shape
    delays = lax.rem(delay_ref[...], frames)
    power = power_ref[...]
    sums = [None] * frames
    for delay in range(frames):
        chosen = (delays == delay).astype(jnp.float32).astype(jnp.bfloat16)
        picked = lax.dot_general(
            power, chosen, (((0,), (1,)), ((), ())), preferred_element_type=jnp.float32
        )
        for frame in range(frames):
            row = (frame + delay) % frames * beams
            term = picked[row : row + beams]
            sums[frame] = term if sums[frame] is None else sums[frame] + term
    for frame in range(frames):
        out_ref[:, frame, :] = sums[frame] * scale


def shift_and_add(power, delays, frames):
    channels, width = power.shape
    beams = width // frames
    return pl.pallas_call(
        functools.partial(shift_kernel, 1.0 / math.sqrt(channels)),
        out_shape=jax.ShapeDtypeStruct((beams, frames, delays.shape[0]), jnp.float32),
        compiler_params=pltpu.CompilerParams(vmem_limit_bytes=8 * 2**20),
        name="shift_and_add",
    )(power, delays)


def plain_spectra(volts, owners, channels):
    frames, antennas, samples = volts.shape
    upper, lower = (jnp.asarray(part) for part in dft_parts(samples, channels))
    x = sum(
        jnp.einsum("krn,fan->kfra", part, volts, preferred_element_type=jnp.float32)
        for part in (upper, lower)
    )
    x = x.astype(jnp.bfloat16).reshape(owners, channels // owners, frames, 2, antennas)
    return x


def plain_beam_power(x, real_weight, imaginary_weight, wides, subs, pols):
    _, own, frames, _, antennas = x.shape
    beams = real_weight.shape[2]
    x = x.reshape(wides, subs, pols, own, frames, 2, antennas)
    x = x.transpose(3, 5, 2, 1, 4, 0, 6).reshape(own, 2, pols * subs * frames, wides * antennas)
    by_re, by_im = (
        jnp.einsum("crfa,cab->rcfb", x, weight, preferred_element_type=jnp.float32)
        for weight in (real_weight, imaginary_weight)
    )
    power = (by_re[0] - by_im[1]) ** 2 + (by_im[0] + by_re[1]) ** 2
    power = power.reshape(own, pols, subs * frames, beams).sum(axis=1)
    power = power - jnp.mean(power, axis=1, keepdims=True)
    targets = wides * subs
    power = power.reshape(own, subs * frames, targets, beams // targets)
    return power.transpose(2, 0, 1, 3).reshape(targets, own, -1).astype(jnp.bfloat16)


def plain_shift_and_add(power, delays, frames):
    channels = power.shape[0]
    power = power.reshape(channels, frames, -1)
    chosen = (delays[None] % frames == jnp.arange(frames)[:, None, None]).astype(jnp.bfloat16)
    picked = jnp.einsum("dtc,cfb->dbft", chosen, power, preferred_element_type=jnp.float32)
    moved = sum(jnp.roll(picked[delay], -delay, axis=1) for delay in range(frames))
    return moved * (1.0 / math.sqrt(channels))


def local(voltages, real_weight, imaginary_weight, delays):
    wides, subs, pols = (lax.axis_size(name) for name in OWNERS)
    owners = wides * subs * pols
    own, _, beams = real_weight.shape
    frames = subs * voltages.shape[2]
    volts = jnp.transpose(voltages[0], (1, 0, 2))
    tiled = (
        own % ROWS == 0
        and voltages.shape[1] % 128 == 0
        and (beams // (wides * subs)) % 32 == 0
        and frames == 4
        and pols == 2
    )
    turn = functools.partial(
        lax.all_to_all, axis_name=OWNERS, split_axis=0, concat_axis=0, tiled=True
    )
    if not tiled:
        x = turn(plain_spectra(volts, owners, own * owners))
        power = plain_beam_power(x, real_weight, imaginary_weight, wides, subs, pols)
        power = jnp.broadcast_to(power[:, None], (wides * subs, pols) + power.shape[1:])
        power = turn(power.reshape(owners, own, -1))
        return plain_shift_and_add(power.reshape(owners * own, -1), delays, frames)
    x = turn(spectra(volts, owners, own * owners))
    power = beam_power(x, real_weight, imaginary_weight, wides, subs, pols)
    power = turn(power.reshape(owners, own, -1))
    return shift_and_add(power.reshape(owners * own, -1), delays, frames)


def solution(mesh):
    placed = (
        P("pol", ("group", "wide"), "sub", None),
        P(OWNERS, None, None),
        P(OWNERS, None, None),
        P("pol", None),
    )
    return jax.shard_map(
        local,
        mesh=mesh,
        in_specs=placed,
        out_specs=P(("group", "wide", "sub"), None, "pol"),
        check_vma=False,
    )
```

```python
import functools
import math

import jax
import jax.numpy as jnp
import ml_dtypes
import numpy as np
from jax import lax
from jax.experimental import pallas as pl
from jax.experimental.pallas import tpu as pltpu
from jax.sharding import PartitionSpec as P

OWNERS = ("wide_high", "wide_low", "sub", "pol")
ROWS = 16
COST = pl.CostEstimate(flops=0, bytes_accessed=0, transcendentals=0)


def dft_parts(samples, channels):
    first = samples // 2 - channels
    bins = first + np.arange(channels, dtype=np.int64)
    turns = bins[:, None] * np.arange(samples, dtype=np.int64)[None, :] % samples
    angles = turns * (2.0 * math.pi / samples)
    exact = np.stack([np.cos(angles), -np.sin(angles)], axis=1) / math.sqrt(samples)
    upper = exact.astype(ml_dtypes.bfloat16)
    lower = (exact - upper.astype(np.float64)).astype(ml_dtypes.bfloat16)
    return upper, lower


def keep_weights(place_ref, first, refs, kept_refs, sem):
    copies = []
    for part, (ref, kept) in enumerate(zip(refs, kept_refs)):
        antennas = kept.shape[2]
        for index in range(kept.shape[0]):
            start = pl.multiple_of(place_ref[first + index] * antennas, antennas)
            copies.append(
                pltpu.make_async_copy(
                    ref.at[:, pl.ds(start, antennas), :], kept.at[index], sem.at[part, index]
                )
            )
    return copies


def dft_kernel(counts, here_ref, table_ref, volt_ref, *refs):
    steps, subs, pols, parts = counts
    weight_refs, refs = refs[:parts], refs[parts:]
    out_refs, refs = refs[: steps * subs], refs[steps * subs :]
    kept_refs, refs = refs[:parts], refs[parts:]
    part_ref, hold_ref, sem = refs[:3]
    frames = volt_ref.shape[0]
    copies = [
        pltpu.make_async_copy(table_ref.at[here_ref[step]], part_ref.at[step], sem.at[step])
        for step in range(steps)
    ]
    keeps = keep_weights(here_ref, 0, weight_refs, kept_refs, refs[-1])
    for copy in copies + keeps:
        copy.start()
    here = here_ref[steps]
    half = part_ref.shape[1] // 2
    for step, copy in enumerate(copies):
        copy.wait()
        for frame in range(frames):
            both = lax.dot_general(
                part_ref[step],
                volt_ref[frame],
                (((1,), (1,)), ((), ())),
                preferred_element_type=jnp.float32,
            )
            spectrum = (both[:half] + both[half:]).astype(jnp.bfloat16)
            hold_ref[step * frames + frame] = spectrum.reshape(
                subs * pols, -1, spectrum.shape[-1]
            )
            for sub in range(subs):
                for pol in range(pols):
                    out_refs[step * subs + sub][pol, frame] = hold_ref[
                        step * frames + frame, (sub * pols + pol) ^ here
                    ]
    for copy in keeps:
        copy.wait()


def spectra(volts, table, here, steps, subs, pols, weights=()):
    frames, antennas, samples = volts.shape
    rows = table.shape[1] // (2 * subs * pols)
    vmem = pl.BlockSpec(memory_space=pltpu.VMEM)
    hbm = pl.BlockSpec(memory_space=pltpu.HBM)
    kept = [
        pltpu.VMEM((steps, weight.shape[0], antennas, weight.shape[2]), weight.dtype)
        for weight in weights
    ]
    pieces = [jax.ShapeDtypeStruct((pols, frames, rows, antennas), jnp.bfloat16)] * (steps * subs)
    outs = pl.pallas_call(
        functools.partial(dft_kernel, (steps, subs, pols, len(weights))),
        in_specs=[pl.BlockSpec(memory_space=pltpu.SMEM), hbm, vmem] + [hbm] * len(weights),
        out_specs=[vmem] * (len(pieces) + len(kept)),
        out_shape=pieces + kept,
        scratch_shapes=[
            pltpu.VMEM((steps,) + table.shape[1:], jnp.bfloat16),
            pltpu.VMEM((steps * frames, subs * pols, rows, antennas), jnp.bfloat16),
            pltpu.SemaphoreType.DMA((steps,)),
            pltpu.SemaphoreType.DMA((2, steps)),
        ],
        compiler_params=pltpu.CompilerParams(vmem_limit_bytes=14 * 2**20),
        name="spectra",
    )(here, table, volts, *weights)
    return list(outs[: len(pieces)]), list(outs[len(pieces) :])


def beam_rows(x_refs, at, pols, order_ref):
    blocks = []
    for pol in range(pols):
        for refs in x_refs:
            frames, _, antennas = refs[pol].shape[1:]
            block = refs[pol][pol, :, at * ROWS : (at + 1) * ROWS, :]
            blocks.append(block.reshape(frames * ROWS, antennas))
    block = jnp.concatenate(blocks, axis=0)
    return jnp.dot(order_ref[...], block, preferred_element_type=jnp.float32).astype(jnp.bfloat16)


def beam_part(lines, half, weights):
    by_re = by_im = None
    for line, re, im in zip(lines, *weights):
        re, im = (
            jnp.dot(line, weight, preferred_element_type=jnp.float32) for weight in (re, im)
        )
        by_re = re if by_re is None else by_re + re
        by_im = im if by_im is None else by_im + im
    return by_re[:half] - by_im[half:], by_im[:half] + by_re[half:]


def first_kernel(counts, place_ref, order_ref, re_ref, im_ref, *refs):
    later, subs, pols = counts
    x_refs = [refs[sub * pols : (sub + 1) * pols] for sub in range(subs)]
    out_ref, re_kept, im_kept, re_held, im_held, sem, kept_sem = refs[subs * pols :]
    groups, group, antennas, _ = re_held.shape
    frames = x_refs[0][0].shape[1]
    half = subs * pols * frames

    start = pl.multiple_of(place_ref[0] * antennas, antennas)
    copies = [
        [
            pltpu.make_async_copy(
                ref.at[pl.ds(at * group, group), pl.ds(start, antennas), :],
                held.at[at],
                sem.at[part, at],
            )
            for part, (ref, held) in enumerate(((re_ref, re_held), (im_ref, im_held)))
        ]
        for at in range(groups)
    ]
    keeps = keep_weights(place_ref, 1, (re_ref, im_ref), (re_kept, im_kept), kept_sem)
    for pair in copies:
        for copy in pair:
            copy.start()
    for copy in keeps:
        copy.start()
    for at in range(groups):
        rows = beam_rows(x_refs, at, pols, order_ref)
        for copy in copies[at]:
            copy.wait()
        for index in range(group):
            line = rows[index * 2 * half : (index + 1) * 2 * half]
            beams = beam_part([line], half, ([re_held[at, index]], [im_held[at, index]]))
            out_ref[at * group + index, :half] = beams[0]
            out_ref[at * group + index, half:] = beams[1]
    for copy in keeps:
        copy.wait()


def last_kernel(counts, place_ref, order_ref, *refs):
    lots, subs, pols = counts
    weight_refs, sum_ref, refs = refs[: 2 * lots], refs[2 * lots], refs[2 * lots + 1 :]
    at_refs = [
        tuple(ref.at[k] for ref in weight_refs[2 * lot : 2 * lot + 2])
        for lot in range(lots)
        for k in range(weight_refs[2 * lot].shape[0])
    ]
    later = len(at_refs)
    x_refs = [
        [refs[(index * subs + sub) * pols :][:pols] for sub in range(subs)]
        for index in range(later)
    ]
    out_ref, power_ref = refs[later * subs * pols :]
    channels = sum_ref.shape[0]
    group = ROWS // 2
    frames = x_refs[0][0][0].shape[1]
    half = subs * pols * frames
    for at in range(channels // group):
        rows = [beam_rows(refs, at, pols, order_ref) for refs in x_refs]
        for index in range(group):
            channel = at * group + index
            weights = [[refs[part][channel] for refs in at_refs] for part in range(2)]
            lines = [row[index * 2 * half : (index + 1) * 2 * half] for row in rows]
            beam_re, beam_im = beam_part(lines, half, weights)
            beam_re = beam_re + sum_ref[channel, :half]
            beam_im = beam_im + sum_ref[channel, half:]
            power = beam_re * beam_re + beam_im * beam_im
            power = sum(power[k * subs * frames : (k + 1) * subs * frames] for k in range(pols))
            power = power - jnp.mean(power, axis=0, keepdims=True)
            for sub in range(subs):
                start = (place_ref[0] ^ sub) * frames
                for frame in range(frames):
                    power_ref[start + frame, channel] = power[sub * frames + frame]
    targets, cores = out_ref.shape[:2]
    beams = power_ref.shape[2] // targets
    for target in range(targets):
        block = jnp.concatenate(
            [power_ref[f, :, target * beams : (target + 1) * beams] for f in range(subs * frames)],
            axis=1,
        ).astype(jnp.bfloat16)
        for core in range(cores):
            out_ref[target, core] = block


def sorting(subs, pols, frames):
    group = ROWS // 2
    count = subs * pols * frames * ROWS
    spot = np.arange(count).reshape(pols, subs, frames, 2, group).transpose(4, 3, 0, 1, 2).reshape(-1)
    order = np.zeros((count, count), np.float32)
    order[np.arange(count), spot] = 1.0
    return jnp.asarray(order, jnp.bfloat16)


def first_beams(xs, place, weights, subs, pols):
    _, frames, _, antennas = xs[0].shape
    channels, _, beams = weights[0].shape
    group = ROWS // 2
    later = place.shape[0] - 1
    vmem = pl.BlockSpec(memory_space=pltpu.VMEM)
    hbm = pl.BlockSpec(memory_space=pltpu.HBM)
    kept = pltpu.VMEM((later, channels, antennas, beams), jnp.bfloat16)
    sums = jax.ShapeDtypeStruct((channels, 2 * subs * pols * frames, beams), jnp.float32)
    held = pltpu.VMEM((channels // group, group, antennas, beams), jnp.bfloat16)
    return pl.pallas_call(
        functools.partial(first_kernel, (later, subs, pols)),
        in_specs=[pl.BlockSpec(memory_space=pltpu.SMEM), vmem, hbm, hbm] + [vmem] * len(xs),
        out_specs=[vmem] * 3,
        out_shape=[sums, kept, kept],
        scratch_shapes=[
            held,
            held,
            pltpu.SemaphoreType.DMA((2, channels // group)),
            pltpu.SemaphoreType.DMA((2, later)),
        ],
        compiler_params=pltpu.CompilerParams(vmem_limit_bytes=14 * 2**20),
        name="first_beams",
    )(place, sorting(subs, pols, frames), *weights, *xs)


def beam_power(xs, place, kept, sums, wides, subs, pols):
    frames = xs[0].shape[1]
    _, channels, _, beams = kept[0].shape
    targets = wides * subs
    width = subs * frames * (beams // targets)
    vmem = pl.BlockSpec(memory_space=pltpu.VMEM)
    return pl.pallas_call(
        functools.partial(last_kernel, (len(kept) // 2, subs, pols)),
        in_specs=[pl.BlockSpec(memory_space=pltpu.SMEM)] + [vmem] * (2 + len(kept) + len(xs)),
        out_specs=vmem,
        out_shape=jax.ShapeDtypeStruct((targets, pols, channels, width), jnp.bfloat16),
        scratch_shapes=[pltpu.VMEM((subs * frames, channels, beams), jnp.float32)],
        compiler_params=pltpu.CompilerParams(vmem_limit_bytes=8 * 2**20),
        name="beam_power",
    )(
        place,
        sorting(subs, pols, frames),
        *(pltpu.with_memory_space_constraint(part, pltpu.VMEM) for part in kept),
        sums,
        *xs,
    )


def exchange(x, offset, names):
    count = math.prod(lax.axis_size(name) for name in names)
    return lax.ppermute(x, names, [(k, k ^ offset) for k in range(count)])


def dft_table(samples, channels, wides, owners):
    own = channels // owners
    group = ROWS // 2

    def order(part):
        part = part.reshape(wides, owners // wides, own // group, group, 2, samples)
        return part.transpose(0, 1, 2, 4, 3, 5).reshape(wides, -1, samples)

    return np.concatenate([order(part) for part in dft_parts(samples, channels)], axis=1)


def shift_kernel(scale, power_ref, delay_ref, out_ref):
    beams, frames, _ = out_ref.shape
    delays = lax.rem(delay_ref[...], frames)
    power = power_ref[...]
    sums = [None] * frames
    for delay in range(frames):
        chosen = (delays == delay).astype(jnp.float32).astype(jnp.bfloat16)
        picked = lax.dot_general(
            power, chosen, (((0,), (1,)), ((), ())), preferred_element_type=jnp.float32
        )
        for frame in range(frames):
            row = (frame + delay) % frames * beams
            term = picked[row : row + beams]
            sums[frame] = term if sums[frame] is None else sums[frame] + term
    for frame in range(frames):
        out_ref[:, frame, :] = sums[frame] * scale


def shift_and_add(power, delays, frames):
    channels, width = power.shape
    beams = width // frames
    return pl.pallas_call(
        functools.partial(shift_kernel, 1.0 / math.sqrt(channels)),
        out_shape=jax.ShapeDtypeStruct((beams, frames, delays.shape[0]), jnp.float32),
        compiler_params=pltpu.CompilerParams(vmem_limit_bytes=8 * 2**20),
        name="shift_and_add",
    )(power, delays)


def plain_spectra(volts, owners, channels):
    frames, antennas, samples = volts.shape
    upper, lower = (jnp.asarray(part) for part in dft_parts(samples, channels))
    x = sum(
        jnp.einsum("krn,fan->kfra", part, volts, preferred_element_type=jnp.float32)
        for part in (upper, lower)
    )
    x = x.astype(jnp.bfloat16).reshape(owners, channels // owners, frames, 2, antennas)
    return x


def plain_beam_power(x, real_weight, imaginary_weight, wides, subs, pols):
    _, own, frames, _, antennas = x.shape
    beams = real_weight.shape[2]
    x = x.reshape(wides, subs, pols, own, frames, 2, antennas)
    x = x.transpose(3, 5, 2, 1, 4, 0, 6).reshape(own, 2, pols * subs * frames, wides * antennas)
    by_re, by_im = (
        jnp.einsum("crfa,cab->rcfb", x, weight, preferred_element_type=jnp.float32)
        for weight in (real_weight, imaginary_weight)
    )
    power = (by_re[0] - by_im[1]) ** 2 + (by_im[0] + by_re[1]) ** 2
    power = power.reshape(own, pols, subs * frames, beams).sum(axis=1)
    power = power - jnp.mean(power, axis=1, keepdims=True)
    targets = wides * subs
    power = power.reshape(own, subs * frames, targets, beams // targets)
    return power.transpose(2, 0, 1, 3).reshape(targets, own, -1).astype(jnp.bfloat16)


def plain_shift_and_add(power, delays, frames):
    channels = power.shape[0]
    power = power.reshape(channels, frames, -1)
    chosen = (delays[None] % frames == jnp.arange(frames)[:, None, None]).astype(jnp.bfloat16)
    picked = jnp.einsum("dtc,cfb->dbft", chosen, power, preferred_element_type=jnp.float32)
    moved = sum(jnp.roll(picked[delay], -delay, axis=1) for delay in range(frames))
    return moved * (1.0 / math.sqrt(channels))


def local(voltages, real_weight, imaginary_weight, delays):
    highs, lows, subs, pols = (lax.axis_size(name) for name in OWNERS)
    wides = highs * lows
    owners = wides * subs * pols
    own, _, beams = real_weight.shape
    frames = subs * voltages.shape[2]
    volts = jnp.transpose(voltages[0], (1, 0, 2))
    tiled = (
        own % ROWS == 0
        and voltages.shape[1] % 128 == 0
        and (beams // (wides * subs)) % 32 == 0
        and frames == 4
        and (wides, subs, pols) == (4, 2, 2)
    )
    turn = functools.partial(
        lax.all_to_all, axis_name=OWNERS, split_axis=0, concat_axis=0, tiled=True
    )
    if not tiled:
        x = turn(plain_spectra(volts, owners, own * owners))
        power = plain_beam_power(x, real_weight, imaginary_weight, wides, subs, pols)
        power = jnp.broadcast_to(power[:, None], (wides * subs, pols) + power.shape[1:])
        power = turn(power.reshape(owners, own, -1))
        return plain_shift_and_add(power.reshape(owners * own, -1), delays, frames)
    high, low, sub, pol = (lax.axis_index(name) for name in OWNERS)
    side, core = lax.axis_size("wide_low"), sub * pols + pol
    table = jnp.asarray(dft_table(voltages.shape[3], own * owners, wides, owners))
    table = pltpu.with_memory_space_constraint(table, pltpu.HBM)
    volts = pltpu.with_memory_space_constraint(volts, pltpu.VMEM)
    weights = [
        pltpu.with_memory_space_constraint(weight, pltpu.HBM)
        for weight in (real_weight, imaginary_weight)
    ]

    def numbers(*values):
        return jnp.stack(values).astype(jnp.int32)

    wide = high * side + low
    offsets = list(range(side, wides)) + list(range(side))[::-1]
    at = [wide ^ offset for offset in offsets]
    far, _ = spectra(volts, table, numbers(*at[:side], core), side, subs, pols)
    volts, _ = lax.optimization_barrier((volts, far[0]))
    near, near_kept = spectra(
        volts, table, numbers(*at[side:], core), side, subs, pols, weights
    )
    moved = []
    for k, piece in enumerate(far + near):
        offset = (offsets[k // subs] * subs + k % subs) * pols
        moved.append(exchange(piece, offset, OWNERS) if offset else piece)

    def both(pieces):
        return [part for mine in pieces for part in (mine, exchange(mine, 1, ("pol",)))]

    first, _ = lax.optimization_barrier((moved[:subs], near[0]))
    sums, *kept = first_beams(both(first), numbers(*at[:side]), weights, subs, pols)
    rest, sums = lax.optimization_barrier((moved[subs:], sums))
    total = beam_power(both(rest), numbers(sub), kept + near_kept, sums, wides, subs, pols)
    power = turn(total.reshape(owners, own, -1))
    return shift_and_add(power.reshape(owners * own, -1), delays, frames)


def solution(mesh):
    names = dict(zip(mesh.axis_names, mesh.devices.shape))
    low = max(1, names["wide"] // 2)
    sizes = (names["group"], names["wide"] // low, low, names["sub"], names["pol"])
    split = jax.sharding.Mesh(mesh.devices.reshape(sizes), ("group",) + OWNERS)
    placed = (
        P("pol", ("group", "wide_high", "wide_low"), "sub", None),
        P(OWNERS, None, None),
        P(OWNERS, None, None),
        P("pol", None),
    )
    return jax.shard_map(
        local,
        mesh=split,
        in_specs=placed,
        out_specs=P(("group", "wide_high", "wide_low", "sub"), None, "pol"),
        check_vma=False,
    )
```

```python
import functools
import math

import jax
import jax.numpy as jnp
import ml_dtypes
import numpy as np
from jax import lax
from jax.experimental import pallas as pl
from jax.experimental.pallas import tpu as pltpu
from jax.sharding import PartitionSpec as P

OWNERS = ("wide_high", "wide_low", "sub", "pol")
ROWS = 16
COST = pl.CostEstimate(flops=0, bytes_accessed=0, transcendentals=0)


def dft_parts(samples, channels):
    first = samples // 2 - channels
    bins = first + np.arange(channels, dtype=np.int64)
    turns = bins[:, None] * np.arange(samples, dtype=np.int64)[None, :] % samples
    angles = turns * (2.0 * math.pi / samples)
    exact = np.stack([np.cos(angles), -np.sin(angles)], axis=1) / math.sqrt(samples)
    upper = exact.astype(ml_dtypes.bfloat16)
    lower = (exact - upper.astype(np.float64)).astype(ml_dtypes.bfloat16)
    return upper, lower


def keep_weights(place_ref, first, refs, kept_refs, sem):
    copies = []
    for part, (ref, kept) in enumerate(zip(refs, kept_refs)):
        antennas = kept.shape[2]
        for index in range(kept.shape[0]):
            start = pl.multiple_of(place_ref[first + index] * antennas, antennas)
            copies.append(
                pltpu.make_async_copy(
                    ref.at[:, pl.ds(start, antennas), :], kept.at[index], sem.at[part, index]
                )
            )
    return copies


def dft_kernel(counts, here_ref, table_ref, volt_ref, *refs):
    steps, subs, pols, parts, first = counts
    weight_refs, refs = refs[:parts], refs[parts:]
    out_refs, refs = refs[: steps * subs], refs[steps * subs :]
    kept_refs, refs = refs[:parts], refs[parts:]
    moved_ref, refs = (refs[0], refs[1:]) if first else (volt_ref, refs)
    part_ref, hold_ref, sem = refs[:3]
    frames = moved_ref.shape[0]
    copies = [
        pltpu.make_async_copy(table_ref.at[here_ref[step]], part_ref.at[step], sem.at[step])
        for step in range(steps)
    ]
    if first:
        raw_ref, raw_sem = refs[3:]
        count = raw_ref.shape[0] // raw_sem.shape[0]
        reads = []
        for index in range(raw_sem.shape[0]):
            rows = pl.ds(index * count, count)
            reads.append(
                pltpu.make_async_copy(volt_ref.at[0, rows], raw_ref.at[rows], raw_sem.at[index])
            )
        for copy in reads + copies:
            copy.start()
        for index, copy in enumerate(reads):
            copy.wait()
            rows = pl.ds(index * count, count)
            moved_ref[:, rows, :] = raw_ref[rows].transpose(1, 0, 2)
        keeps = []
    else:
        keeps = keep_weights(here_ref, steps - kept_refs[0].shape[0], weight_refs, kept_refs, refs[3])
        for copy in copies + keeps:
            copy.start()
    here = here_ref[steps]
    half = part_ref.shape[1] // 2
    for step, copy in enumerate(copies):
        copy.wait()
        for frame in range(frames):
            both = lax.dot_general(
                part_ref[step],
                moved_ref[frame],
                (((1,), (1,)), ((), ())),
                preferred_element_type=jnp.float32,
            )
            spectrum = (both[:half] + both[half:]).astype(jnp.bfloat16)
            hold_ref[step * frames + frame] = spectrum.reshape(
                subs * pols, -1, spectrum.shape[-1]
            )
            for sub in range(subs):
                for pol in range(pols):
                    out_refs[step * subs + sub][pol, frame] = hold_ref[
                        step * frames + frame, (sub * pols + pol) ^ here
                    ]
    for copy in keeps:
        copy.wait()


def spectra(volts, table, here, steps, subs, pols, weights=(), keep=0):
    first = volts.ndim == 4
    frames, antennas = volts.shape[:2] if not first else volts.shape[2:0:-1]
    samples = volts.shape[-1]
    rows = table.shape[1] // (2 * subs * pols)
    vmem = pl.BlockSpec(memory_space=pltpu.VMEM)
    hbm = pl.BlockSpec(memory_space=pltpu.HBM)
    kept = [
        pltpu.VMEM((keep, weight.shape[0], antennas, weight.shape[2]), weight.dtype)
        for weight in weights
    ]
    pieces = [jax.ShapeDtypeStruct((pols, frames, rows, antennas), jnp.bfloat16)] * (steps * subs)
    scratch = [
        pltpu.VMEM((steps,) + table.shape[1:], jnp.bfloat16),
        pltpu.VMEM((steps * frames, subs * pols, rows, antennas), jnp.bfloat16),
        pltpu.SemaphoreType.DMA((steps,)),
    ]
    if first:
        kept.append(pltpu.VMEM((frames, antennas, samples), volts.dtype))
        scratch.append(pltpu.VMEM((antennas, frames, samples), volts.dtype))
        scratch.append(pltpu.SemaphoreType.DMA((4,)))
        volts = pltpu.with_memory_space_constraint(volts, pltpu.HBM)
    else:
        scratch.append(pltpu.SemaphoreType.DMA((2, keep)))
        volts = pltpu.with_memory_space_constraint(volts, pltpu.VMEM)
    outs = pl.pallas_call(
        functools.partial(dft_kernel, (steps, subs, pols, len(weights), first)),
        in_specs=[pl.BlockSpec(memory_space=pltpu.SMEM), hbm, hbm if first else vmem]
        + [hbm] * len(weights),
        out_specs=[vmem] * (len(pieces) + len(kept)),
        out_shape=pieces + kept,
        scratch_shapes=scratch,
        compiler_params=pltpu.CompilerParams(vmem_limit_bytes=12 * 2**20),
        name="spectra",
    )(here, table, volts, *weights)
    return list(outs[: len(pieces)]), list(outs[len(pieces) :])


def beam_rows(x_refs, at, pols, order_ref):
    blocks = []
    for pol in range(pols):
        for refs in x_refs:
            frames, _, antennas = refs[pol].shape[1:]
            block = refs[pol][0, :, at * ROWS : (at + 1) * ROWS, :]
            blocks.append(block.reshape(frames * ROWS, antennas))
    block = jnp.concatenate(blocks, axis=0)
    return jnp.dot(order_ref[...], block, preferred_element_type=jnp.float32).astype(jnp.bfloat16)


def beam_part(lines, half, weights):
    by_re = by_im = None
    for line, re, im in zip(lines, *weights):
        re, im = (
            jnp.dot(line, weight, preferred_element_type=jnp.float32) for weight in (re, im)
        )
        by_re = re if by_re is None else by_re + re
        by_im = im if by_im is None else by_im + im
    return by_re[:half] - by_im[half:], by_im[:half] + by_re[half:]


def first_kernel(counts, place_ref, order_ref, re_ref, im_ref, *refs):
    later, subs, pols = counts
    x_refs = [refs[sub * pols : (sub + 1) * pols] for sub in range(subs)]
    out_ref, re_kept, im_kept, re_held, im_held, sem, kept_sem = refs[subs * pols :]
    groups, group, antennas, _ = re_held.shape
    frames = x_refs[0][0].shape[1]
    half = subs * pols * frames

    start = pl.multiple_of(place_ref[0] * antennas, antennas)
    copies = [
        [
            pltpu.make_async_copy(
                ref.at[pl.ds(at * group, group), pl.ds(start, antennas), :],
                held.at[at],
                sem.at[part, at],
            )
            for part, (ref, held) in enumerate(((re_ref, re_held), (im_ref, im_held)))
        ]
        for at in range(groups)
    ]
    keeps = keep_weights(place_ref, 1, (re_ref, im_ref), (re_kept, im_kept), kept_sem)
    for pair in copies:
        for copy in pair:
            copy.start()
    for copy in keeps:
        copy.start()
    for at in range(groups):
        rows = beam_rows(x_refs, at, pols, order_ref)
        for copy in copies[at]:
            copy.wait()
        for index in range(group):
            line = rows[index * 2 * half : (index + 1) * 2 * half]
            beams = beam_part([line], half, ([re_held[at, index]], [im_held[at, index]]))
            out_ref[at * group + index, :half] = beams[0]
            out_ref[at * group + index, half:] = beams[1]
    for copy in keeps:
        copy.wait()


def last_kernel(counts, place_ref, order_ref, *refs):
    lots, subs, pols = counts
    weight_refs, sum_ref, refs = refs[: 2 * lots], refs[2 * lots], refs[2 * lots + 1 :]
    at_refs = [
        tuple(ref.at[k] for ref in weight_refs[2 * lot : 2 * lot + 2])
        for lot in range(lots)
        for k in range(weight_refs[2 * lot].shape[0])
    ]
    later = len(at_refs)
    x_refs = [
        [refs[(index * subs + sub) * pols :][:pols] for sub in range(subs)]
        for index in range(later)
    ]
    out_ref, power_ref = refs[later * subs * pols :]
    channels = sum_ref.shape[0]
    group = ROWS // 2
    frames = x_refs[0][0][0].shape[1]
    half = subs * pols * frames
    for at in range(channels // group):
        rows = [beam_rows(refs, at, pols, order_ref) for refs in x_refs]
        for index in range(group):
            channel = at * group + index
            weights = [[refs[part][channel] for refs in at_refs] for part in range(2)]
            lines = [row[index * 2 * half : (index + 1) * 2 * half] for row in rows]
            beam_re, beam_im = beam_part(lines, half, weights)
            beam_re = beam_re + sum_ref[channel, :half]
            beam_im = beam_im + sum_ref[channel, half:]
            power = beam_re * beam_re + beam_im * beam_im
            power = sum(power[k * subs * frames : (k + 1) * subs * frames] for k in range(pols))
            power = power - jnp.mean(power, axis=0, keepdims=True)
            for sub in range(subs):
                start = (place_ref[0] ^ sub) * frames
                for frame in range(frames):
                    power_ref[start + frame, channel] = power[sub * frames + frame]
    targets, cores = out_ref.shape[:2]
    beams = power_ref.shape[2] // targets
    for target in range(targets):
        block = jnp.concatenate(
            [power_ref[f, :, target * beams : (target + 1) * beams] for f in range(subs * frames)],
            axis=1,
        ).astype(jnp.bfloat16)
        for core in range(cores):
            out_ref[target, core] = block


def sorting(subs, pols, frames):
    group = ROWS // 2
    count = subs * pols * frames * ROWS
    spot = np.arange(count).reshape(pols, subs, frames, 2, group).transpose(4, 3, 0, 1, 2).reshape(-1)
    order = np.zeros((count, count), np.float32)
    order[np.arange(count), spot] = 1.0
    return jnp.asarray(order, jnp.bfloat16)


def first_beams(xs, place, weights, subs, pols):
    _, frames, _, antennas = xs[0].shape
    channels, _, beams = weights[0].shape
    group = ROWS // 2
    later = place.shape[0] - 1
    vmem = pl.BlockSpec(memory_space=pltpu.VMEM)
    hbm = pl.BlockSpec(memory_space=pltpu.HBM)
    kept = pltpu.VMEM((later, channels, antennas, beams), jnp.bfloat16)
    sums = jax.ShapeDtypeStruct((channels, 2 * subs * pols * frames, beams), jnp.float32)
    held = pltpu.VMEM((channels // group, group, antennas, beams), jnp.bfloat16)
    return pl.pallas_call(
        functools.partial(first_kernel, (later, subs, pols)),
        in_specs=[pl.BlockSpec(memory_space=pltpu.SMEM), vmem, hbm, hbm] + [vmem] * len(xs),
        out_specs=[vmem] * 3,
        out_shape=[sums, kept, kept],
        scratch_shapes=[
            held,
            held,
            pltpu.SemaphoreType.DMA((2, channels // group)),
            pltpu.SemaphoreType.DMA((2, later)),
        ],
        compiler_params=pltpu.CompilerParams(vmem_limit_bytes=12 * 2**20),
        cost_estimate=pl.CostEstimate(flops=4*10**10, bytes_accessed=4*10**8, transcendentals=0),
        name="first_beams",
    )(place, sorting(subs, pols, frames), *weights, *xs)


def beam_power(xs, place, kept, sums, wides, subs, pols):
    frames = xs[0].shape[1]
    _, channels, _, beams = kept[0].shape
    targets = wides * subs
    width = subs * frames * (beams // targets)
    vmem = pl.BlockSpec(memory_space=pltpu.VMEM)
    return pl.pallas_call(
        functools.partial(last_kernel, (len(kept) // 2, subs, pols)),
        in_specs=[pl.BlockSpec(memory_space=pltpu.SMEM)] + [vmem] * (2 + len(kept) + len(xs)),
        out_specs=vmem,
        out_shape=jax.ShapeDtypeStruct((targets, pols, channels, width), jnp.bfloat16),
        scratch_shapes=[pltpu.VMEM((subs * frames, channels, beams), jnp.float32)],
        compiler_params=pltpu.CompilerParams(vmem_limit_bytes=8 * 2**20),
        name="beam_power",
    )(
        place,
        sorting(subs, pols, frames),
        *(pltpu.with_memory_space_constraint(part, pltpu.VMEM) for part in kept),
        sums,
        *xs,
    )


def exchange(x, offset, names):
    count = math.prod(lax.axis_size(name) for name in names)
    return lax.ppermute(x, names, [(k, k ^ offset) for k in range(count)])


def dft_table(samples, channels, wides, owners):
    own = channels // owners
    group = ROWS // 2

    def order(part):
        part = part.reshape(wides, owners // wides, own // group, group, 2, samples)
        return part.transpose(0, 1, 2, 4, 3, 5).reshape(wides, -1, samples)

    return np.concatenate([order(part) for part in dft_parts(samples, channels)], axis=1)


def shift_kernel(scale, power_ref, delay_ref, out_ref):
    beams, frames, _ = out_ref.shape
    delays = lax.rem(delay_ref[...], frames)
    power = power_ref[...]
    sums = [None] * frames
    for delay in range(frames):
        chosen = (delays == delay).astype(jnp.float32).astype(jnp.bfloat16)
        picked = lax.dot_general(
            power, chosen, (((0,), (1,)), ((), ())), preferred_element_type=jnp.float32
        )
        for frame in range(frames):
            row = (frame + delay) % frames * beams
            term = picked[row : row + beams]
            sums[frame] = term if sums[frame] is None else sums[frame] + term
    for frame in range(frames):
        out_ref[:, frame, :] = sums[frame] * scale


def shift_and_add(power, delays, frames):
    channels, width = power.shape
    beams = width // frames
    return pl.pallas_call(
        functools.partial(shift_kernel, 1.0 / math.sqrt(channels)),
        out_shape=jax.ShapeDtypeStruct((beams, frames, delays.shape[0]), jnp.float32),
        compiler_params=pltpu.CompilerParams(vmem_limit_bytes=8 * 2**20),
        name="shift_and_add",
    )(power, delays)


def plain_spectra(volts, owners, channels):
    frames, antennas, samples = volts.shape
    upper, lower = (jnp.asarray(part) for part in dft_parts(samples, channels))
    x = sum(
        jnp.einsum("krn,fan->kfra", part, volts, preferred_element_type=jnp.float32)
        for part in (upper, lower)
    )
    x = x.astype(jnp.bfloat16).reshape(owners, channels // owners, frames, 2, antennas)
    return x


def plain_beam_power(x, real_weight, imaginary_weight, wides, subs, pols):
    _, own, frames, _, antennas = x.shape
    beams = real_weight.shape[2]
    x = x.reshape(wides, subs, pols, own, frames, 2, antennas)
    x = x.transpose(3, 5, 2, 1, 4, 0, 6).reshape(own, 2, pols * subs * frames, wides * antennas)
    by_re, by_im = (
        jnp.einsum("crfa,cab->rcfb", x, weight, preferred_element_type=jnp.float32)
        for weight in (real_weight, imaginary_weight)
    )
    power = (by_re[0] - by_im[1]) ** 2 + (by_im[0] + by_re[1]) ** 2
    power = power.reshape(own, pols, subs * frames, beams).sum(axis=1)
    power = power - jnp.mean(power, axis=1, keepdims=True)
    targets = wides * subs
    power = power.reshape(own, subs * frames, targets, beams // targets)
    return power.transpose(2, 0, 1, 3).reshape(targets, own, -1).astype(jnp.bfloat16)


def plain_shift_and_add(power, delays, frames):
    channels = power.shape[0]
    power = power.reshape(channels, frames, -1)
    chosen = (delays[None] % frames == jnp.arange(frames)[:, None, None]).astype(jnp.bfloat16)
    picked = jnp.einsum("dtc,cfb->dbft", chosen, power, preferred_element_type=jnp.float32)
    moved = sum(jnp.roll(picked[delay], -delay, axis=1) for delay in range(frames))
    return moved * (1.0 / math.sqrt(channels))


def local(voltages, real_weight, imaginary_weight, delays):
    highs, lows, subs, pols = (lax.axis_size(name) for name in OWNERS)
    wides = highs * lows
    owners = wides * subs * pols
    own, _, beams = real_weight.shape
    frames = subs * voltages.shape[2]
    tiled = (
        own % ROWS == 0
        and voltages.shape[1] % 128 == 0
        and (beams // (wides * subs)) % 32 == 0
        and frames == 4
        and (wides, subs, pols) == (4, 2, 2)
    )
    turn = functools.partial(
        lax.all_to_all, axis_name=OWNERS, split_axis=0, concat_axis=0, tiled=True
    )
    if not tiled:
        volts = jnp.transpose(voltages[0], (1, 0, 2))
        x = turn(plain_spectra(volts, owners, own * owners))
        power = plain_beam_power(x, real_weight, imaginary_weight, wides, subs, pols)
        power = jnp.broadcast_to(power[:, None], (wides * subs, pols) + power.shape[1:])
        power = turn(power.reshape(owners, own, -1))
        return plain_shift_and_add(power.reshape(owners * own, -1), delays, frames)
    high, low, sub, pol = (lax.axis_index(name) for name in OWNERS)
    side, core = lax.axis_size("wide_low"), sub * pols + pol
    table = jnp.asarray(dft_table(voltages.shape[3], own * owners, wides, owners))
    table = pltpu.with_memory_space_constraint(table, pltpu.HBM)
    weights = [
        pltpu.with_memory_space_constraint(weight, pltpu.HBM)
        for weight in (real_weight, imaginary_weight)
    ]

    def numbers(*values):
        return jnp.stack(values).astype(jnp.int32)

    wide = high * side + low
    offsets = list(range(side, wides)) + list(range(side))[::-1]
    at = [wide ^ offset for offset in offsets]
    far, (volts,) = spectra(voltages, table, numbers(at[0], core), 1, subs, pols)
    near, near_kept = spectra(
        volts, table, numbers(*at[1:], core), wides - 1, subs, pols, weights, side
    )
    moved = []
    for k, piece in enumerate(far + near):
        offset = (offsets[k // subs] * subs + k % subs) * pols
        moved.append(exchange(piece, offset, OWNERS) if offset else piece)

    def both(pieces):
        return [part for mine in pieces for part in (mine, exchange(mine[1:], 1, ("pol",)))]

    first, _ = lax.optimization_barrier((moved[:subs], near[0]))
    sums, *kept = first_beams(both(first), numbers(*at[:side]), weights, subs, pols)
    rest, sums = lax.optimization_barrier((moved[subs:], sums))
    total = beam_power(both(rest), numbers(sub), kept + near_kept, sums, wides, subs, pols)
    power = turn(total.reshape(owners, own, -1))
    return shift_and_add(power.reshape(owners * own, -1), delays, frames)


def solution(mesh):
    names = dict(zip(mesh.axis_names, mesh.devices.shape))
    low = max(1, names["wide"] // 2)
    sizes = (names["group"], names["wide"] // low, low, names["sub"], names["pol"])
    split = jax.sharding.Mesh(mesh.devices.reshape(sizes), ("group",) + OWNERS)
    placed = (
        P("pol", ("group", "wide_high", "wide_low"), "sub", None),
        P(OWNERS, None, None),
        P(OWNERS, None, None),
        P("pol", None),
    )
    return jax.shard_map(
        local,
        mesh=split,
        in_specs=placed,
        out_specs=P(("group", "wide_high", "wide_low", "sub"), None, "pol"),
        check_vma=False,
    )
```

```python
import functools
import math

import jax
import jax.numpy as jnp
import ml_dtypes
import numpy as np
from jax import lax
from jax.experimental import pallas as pl
from jax.experimental.pallas import tpu as pltpu
from jax.sharding import PartitionSpec as P

OWNERS = ("wide_high", "wide_low", "sub", "pol")
ROWS = 16
COST = pl.CostEstimate(flops=0, bytes_accessed=0, transcendentals=0)


def dft_parts(samples, channels):
    first = samples // 2 - channels
    bins = first + np.arange(channels, dtype=np.int64)
    turns = bins[:, None] * np.arange(samples, dtype=np.int64)[None, :] % samples
    angles = turns * (2.0 * math.pi / samples)
    exact = np.stack([np.cos(angles), -np.sin(angles)], axis=1) / math.sqrt(samples)
    upper = exact.astype(ml_dtypes.bfloat16)
    lower = (exact - upper.astype(np.float64)).astype(ml_dtypes.bfloat16)
    return upper, lower


def keep_weights(place_ref, first, refs, kept_refs, sem):
    copies = []
    for part, (ref, kept) in enumerate(zip(refs, kept_refs)):
        antennas = kept.shape[2]
        for index in range(kept.shape[0]):
            start = pl.multiple_of(place_ref[first + index] * antennas, antennas)
            copies.append(
                pltpu.make_async_copy(
                    ref.at[:, pl.ds(start, antennas), :], kept.at[index], sem.at[part, index]
                )
            )
    return copies


def dft_kernel(counts, here_ref, table_ref, volt_ref, *refs):
    steps, subs, pols, parts, first = counts
    weight_refs, refs = refs[:parts], refs[parts:]
    out_refs, refs = refs[: steps * subs], refs[steps * subs :]
    kept_refs, refs = refs[:parts], refs[parts:]
    moved_ref, refs = (refs[0], refs[1:]) if first else (volt_ref, refs)
    part_ref, hold_ref, sem = refs[:3]
    frames = moved_ref.shape[0]
    copies = [
        pltpu.make_async_copy(table_ref.at[here_ref[step]], part_ref.at[step], sem.at[step])
        for step in range(steps)
    ]
    if first:
        raw_ref, raw_sem = refs[3:]
        count = raw_ref.shape[0] // raw_sem.shape[0]
        reads = []
        for index in range(raw_sem.shape[0]):
            rows = pl.ds(index * count, count)
            reads.append(
                pltpu.make_async_copy(volt_ref.at[0, rows], raw_ref.at[rows], raw_sem.at[index])
            )
        for copy in reads + copies:
            copy.start()
        for index, copy in enumerate(reads):
            copy.wait()
            rows = pl.ds(index * count, count)
            moved_ref[:, rows, :] = raw_ref[rows].transpose(1, 0, 2)
        keeps = []
    else:
        keeps = keep_weights(here_ref, steps - kept_refs[0].shape[0], weight_refs, kept_refs, refs[3])
        for copy in copies + keeps:
            copy.start()
    here = here_ref[steps]
    half = part_ref.shape[1] // 2
    for step, copy in enumerate(copies):
        copy.wait()
        for frame in range(frames):
            both = lax.dot_general(
                part_ref[step],
                moved_ref[frame],
                (((1,), (1,)), ((), ())),
                preferred_element_type=jnp.float32,
            )
            spectrum = (both[:half] + both[half:]).astype(jnp.bfloat16)
            hold_ref[step * frames + frame] = spectrum.reshape(
                subs * pols, -1, spectrum.shape[-1]
            )
            for sub in range(subs):
                for pol in range(pols):
                    out_refs[step * subs + sub][pol, frame] = hold_ref[
                        step * frames + frame, (sub * pols + pol) ^ here
                    ]
    for copy in keeps:
        copy.wait()


def spectra(volts, table, here, steps, subs, pols, weights=(), keep=0):
    first = volts.ndim == 4
    frames, antennas = volts.shape[:2] if not first else volts.shape[2:0:-1]
    samples = volts.shape[-1]
    rows = table.shape[1] // (2 * subs * pols)
    vmem = pl.BlockSpec(memory_space=pltpu.VMEM)
    hbm = pl.BlockSpec(memory_space=pltpu.HBM)
    kept = [
        pltpu.VMEM((keep, weight.shape[0], antennas, weight.shape[2]), weight.dtype)
        for weight in weights
    ]
    pieces = [jax.ShapeDtypeStruct((pols, frames, rows, antennas), jnp.bfloat16)] * (steps * subs)
    scratch = [
        pltpu.VMEM((steps,) + table.shape[1:], jnp.bfloat16),
        pltpu.VMEM((steps * frames, subs * pols, rows, antennas), jnp.bfloat16),
        pltpu.SemaphoreType.DMA((steps,)),
    ]
    if first:
        kept.append(pltpu.VMEM((frames, antennas, samples), volts.dtype))
        scratch.append(pltpu.VMEM((antennas, frames, samples), volts.dtype))
        scratch.append(pltpu.SemaphoreType.DMA((4,)))
        volts = pltpu.with_memory_space_constraint(volts, pltpu.HBM)
    else:
        scratch.append(pltpu.SemaphoreType.DMA((2, keep)))
        volts = pltpu.with_memory_space_constraint(volts, pltpu.VMEM)
    outs = pl.pallas_call(
        functools.partial(dft_kernel, (steps, subs, pols, len(weights), first)),
        in_specs=[pl.BlockSpec(memory_space=pltpu.SMEM), hbm, hbm if first else vmem]
        + [hbm] * len(weights),
        out_specs=[vmem] * (len(pieces) + len(kept)),
        out_shape=pieces + kept,
        scratch_shapes=scratch,
        compiler_params=pltpu.CompilerParams(vmem_limit_bytes=12 * 2**20),
        name="spectra",
    )(here, table, volts, *weights)
    return list(outs[: len(pieces)]), list(outs[len(pieces) :])


def beam_rows(x_refs, index, subs, at, order_ref):
    blocks = []
    for own in (True, False):
        for piece in range(index * subs, (index + 1) * subs):
            if own:
                ref, lead = x_refs[piece], 0
            elif len(x_refs) % 2:
                ref, lead = x_refs[-1], piece
            else:
                ref, lead = x_refs[len(x_refs) // 2 + piece], 0
            frames, _, antennas = ref.shape[1:]
            block = ref[lead, :, at * ROWS : (at + 1) * ROWS, :]
            blocks.append(block.reshape(frames * ROWS, antennas))
    block = jnp.concatenate(blocks, axis=0)
    return jnp.dot(order_ref[...], block, preferred_element_type=jnp.float32).astype(jnp.bfloat16)


def beam_part(lines, half, weights):
    by_re = by_im = None
    for line, re, im in zip(lines, *weights):
        re, im = (
            jnp.dot(line, weight, preferred_element_type=jnp.float32) for weight in (re, im)
        )
        by_re = re if by_re is None else by_re + re
        by_im = im if by_im is None else by_im + im
    return by_re[:half] - by_im[half:], by_im[:half] + by_re[half:]


def first_kernel(counts, place_ref, order_ref, re_ref, im_ref, *refs):
    later, subs, pols = counts
    x_refs = refs[: subs * pols]
    out_ref, re_kept, im_kept, re_held, im_held, sem, kept_sem = refs[subs * pols :]
    groups, group, antennas, _ = re_held.shape
    frames = x_refs[0].shape[1]
    half = subs * pols * frames

    start = pl.multiple_of(place_ref[0] * antennas, antennas)
    copies = [
        [
            pltpu.make_async_copy(
                ref.at[pl.ds(at * group, group), pl.ds(start, antennas), :],
                held.at[at],
                sem.at[part, at],
            )
            for part, (ref, held) in enumerate(((re_ref, re_held), (im_ref, im_held)))
        ]
        for at in range(groups)
    ]
    keeps = keep_weights(place_ref, 1, (re_ref, im_ref), (re_kept, im_kept), kept_sem)
    for pair in copies:
        for copy in pair:
            copy.start()
    for copy in keeps:
        copy.start()
    for at in range(groups):
        rows = beam_rows(x_refs, 0, subs, at, order_ref)
        for copy in copies[at]:
            copy.wait()
        for index in range(group):
            line = rows[index * 2 * half : (index + 1) * 2 * half]
            beams = beam_part([line], half, ([re_held[at, index]], [im_held[at, index]]))
            out_ref[at * group + index, :half] = beams[0]
            out_ref[at * group + index, half:] = beams[1]
    for copy in keeps:
        copy.wait()


def last_kernel(counts, place_ref, order_ref, *refs):
    lots, subs, pols = counts
    weight_refs, sum_ref, refs = refs[: 2 * lots], refs[2 * lots], refs[2 * lots + 1 :]
    at_refs = [
        tuple(ref.at[k] for ref in weight_refs[2 * lot : 2 * lot + 2])
        for lot in range(lots)
        for k in range(weight_refs[2 * lot].shape[0])
    ]
    x_refs, (out_ref, power_ref) = refs[:-2], refs[-2:]
    channels = sum_ref.shape[0]
    group = ROWS // 2
    frames = x_refs[0].shape[1]
    half = subs * pols * frames
    for at in range(channels // group):
        rows = [beam_rows(x_refs, k, subs, at, order_ref) for k in range(len(at_refs))]
        for index in range(group):
            channel = at * group + index
            weights = [[refs[part][channel] for refs in at_refs] for part in range(2)]
            lines = [row[index * 2 * half : (index + 1) * 2 * half] for row in rows]
            beam_re, beam_im = beam_part(lines, half, weights)
            beam_re = beam_re + sum_ref[channel, :half]
            beam_im = beam_im + sum_ref[channel, half:]
            power = beam_re * beam_re + beam_im * beam_im
            power = sum(power[k * subs * frames : (k + 1) * subs * frames] for k in range(pols))
            power = power - jnp.mean(power, axis=0, keepdims=True)
            for sub in range(subs):
                start = (place_ref[0] ^ sub) * frames
                for frame in range(frames):
                    power_ref[start + frame, channel] = power[sub * frames + frame]
    targets, cores = out_ref.shape[:2]
    beams = power_ref.shape[2] // targets
    for target in range(targets):
        block = jnp.concatenate(
            [power_ref[f, :, target * beams : (target + 1) * beams] for f in range(subs * frames)],
            axis=1,
        ).astype(jnp.bfloat16)
        for core in range(cores):
            out_ref[target, core] = block


def sorting(subs, pols, frames):
    group = ROWS // 2
    count = subs * pols * frames * ROWS
    spot = np.arange(count).reshape(pols, subs, frames, 2, group).transpose(4, 3, 0, 1, 2).reshape(-1)
    order = np.zeros((count, count), np.float32)
    order[np.arange(count), spot] = 1.0
    return jnp.asarray(order, jnp.bfloat16)


def first_beams(xs, place, weights, subs, pols):
    _, frames, _, antennas = xs[0].shape
    channels, _, beams = weights[0].shape
    group = ROWS // 2
    later = place.shape[0] - 1
    vmem = pl.BlockSpec(memory_space=pltpu.VMEM)
    hbm = pl.BlockSpec(memory_space=pltpu.HBM)
    kept = pltpu.VMEM((later, channels, antennas, beams), jnp.bfloat16)
    sums = jax.ShapeDtypeStruct((channels, 2 * subs * pols * frames, beams), jnp.float32)
    held = pltpu.VMEM((channels // group, group, antennas, beams), jnp.bfloat16)
    return pl.pallas_call(
        functools.partial(first_kernel, (later, subs, pols)),
        in_specs=[pl.BlockSpec(memory_space=pltpu.SMEM), vmem, hbm, hbm] + [vmem] * len(xs),
        out_specs=[vmem] * 3,
        out_shape=[sums, kept, kept],
        scratch_shapes=[
            held,
            held,
            pltpu.SemaphoreType.DMA((2, channels // group)),
            pltpu.SemaphoreType.DMA((2, later)),
        ],
        compiler_params=pltpu.CompilerParams(vmem_limit_bytes=12 * 2**20),
        cost_estimate=pl.CostEstimate(flops=4*10**10, bytes_accessed=4*10**8, transcendentals=0),
        name="first_beams",
    )(place, sorting(subs, pols, frames), *weights, *xs)


def beam_power(xs, place, kept, sums, wides, subs, pols):
    frames = xs[0].shape[1]
    _, channels, _, beams = kept[0].shape
    targets = wides * subs
    width = subs * frames * (beams // targets)
    vmem = pl.BlockSpec(memory_space=pltpu.VMEM)
    return pl.pallas_call(
        functools.partial(last_kernel, (len(kept) // 2, subs, pols)),
        in_specs=[pl.BlockSpec(memory_space=pltpu.SMEM)] + [vmem] * (2 + len(kept) + len(xs)),
        out_specs=vmem,
        out_shape=jax.ShapeDtypeStruct((targets, pols, channels, width), jnp.bfloat16),
        scratch_shapes=[pltpu.VMEM((subs * frames, channels, beams), jnp.float32)],
        compiler_params=pltpu.CompilerParams(vmem_limit_bytes=8 * 2**20),
        name="beam_power",
    )(
        place,
        sorting(subs, pols, frames),
        *(pltpu.with_memory_space_constraint(part, pltpu.VMEM) for part in kept),
        sums,
        *xs,
    )


def exchange(x, offset, names):
    count = math.prod(lax.axis_size(name) for name in names)
    return lax.ppermute(x, names, [(k, k ^ offset) for k in range(count)])


def dft_table(samples, channels, wides, owners):
    own = channels // owners
    group = ROWS // 2

    def order(part):
        part = part.reshape(wides, owners // wides, own // group, group, 2, samples)
        return part.transpose(0, 1, 2, 4, 3, 5).reshape(wides, -1, samples)

    return np.concatenate([order(part) for part in dft_parts(samples, channels)], axis=1)


def shift_kernel(scale, power_ref, delay_ref, out_ref):
    beams, frames, _ = out_ref.shape
    delays = lax.rem(delay_ref[...], frames)
    power = power_ref[...]
    sums = [None] * frames
    for delay in range(frames):
        chosen = (delays == delay).astype(jnp.float32).astype(jnp.bfloat16)
        picked = lax.dot_general(
            power, chosen, (((0,), (1,)), ((), ())), preferred_element_type=jnp.float32
        )
        for frame in range(frames):
            row = (frame + delay) % frames * beams
            term = picked[row : row + beams]
            sums[frame] = term if sums[frame] is None else sums[frame] + term
    for frame in range(frames):
        out_ref[:, frame, :] = sums[frame] * scale


def shift_and_add(power, delays, frames):
    channels, width = power.shape
    beams = width // frames
    return pl.pallas_call(
        functools.partial(shift_kernel, 1.0 / math.sqrt(channels)),
        out_shape=jax.ShapeDtypeStruct((beams, frames, delays.shape[0]), jnp.float32),
        compiler_params=pltpu.CompilerParams(vmem_limit_bytes=8 * 2**20),
        name="shift_and_add",
    )(power, delays)


def plain_spectra(volts, owners, channels):
    frames, antennas, samples = volts.shape
    upper, lower = (jnp.asarray(part) for part in dft_parts(samples, channels))
    x = sum(
        jnp.einsum("krn,fan->kfra", part, volts, preferred_element_type=jnp.float32)
        for part in (upper, lower)
    )
    x = x.astype(jnp.bfloat16).reshape(owners, channels // owners, frames, 2, antennas)
    return x


def plain_beam_power(x, real_weight, imaginary_weight, wides, subs, pols):
    _, own, frames, _, antennas = x.shape
    beams = real_weight.shape[2]
    x = x.reshape(wides, subs, pols, own, frames, 2, antennas)
    x = x.transpose(3, 5, 2, 1, 4, 0, 6).reshape(own, 2, pols * subs * frames, wides * antennas)
    by_re, by_im = (
        jnp.einsum("crfa,cab->rcfb", x, weight, preferred_element_type=jnp.float32)
        for weight in (real_weight, imaginary_weight)
    )
    power = (by_re[0] - by_im[1]) ** 2 + (by_im[0] + by_re[1]) ** 2
    power = power.reshape(own, pols, subs * frames, beams).sum(axis=1)
    power = power - jnp.mean(power, axis=1, keepdims=True)
    targets = wides * subs
    power = power.reshape(own, subs * frames, targets, beams // targets)
    return power.transpose(2, 0, 1, 3).reshape(targets, own, -1).astype(jnp.bfloat16)


def plain_shift_and_add(power, delays, frames):
    channels = power.shape[0]
    power = power.reshape(channels, frames, -1)
    chosen = (delays[None] % frames == jnp.arange(frames)[:, None, None]).astype(jnp.bfloat16)
    picked = jnp.einsum("dtc,cfb->dbft", chosen, power, preferred_element_type=jnp.float32)
    moved = sum(jnp.roll(picked[delay], -delay, axis=1) for delay in range(frames))
    return moved * (1.0 / math.sqrt(channels))


def local(voltages, real_weight, imaginary_weight, delays):
    highs, lows, subs, pols = (lax.axis_size(name) for name in OWNERS)
    wides = highs * lows
    owners = wides * subs * pols
    own, _, beams = real_weight.shape
    frames = subs * voltages.shape[2]
    tiled = (
        own % ROWS == 0
        and voltages.shape[1] % 128 == 0
        and (beams // (wides * subs)) % 32 == 0
        and frames == 4
        and (wides, subs, pols) == (4, 2, 2)
    )
    turn = functools.partial(
        lax.all_to_all, axis_name=OWNERS, split_axis=0, concat_axis=0, tiled=True
    )
    if not tiled:
        volts = jnp.transpose(voltages[0], (1, 0, 2))
        x = turn(plain_spectra(volts, owners, own * owners))
        power = plain_beam_power(x, real_weight, imaginary_weight, wides, subs, pols)
        power = jnp.broadcast_to(power[:, None], (wides * subs, pols) + power.shape[1:])
        power = turn(power.reshape(owners, own, -1))
        return plain_shift_and_add(power.reshape(owners * own, -1), delays, frames)
    high, low, sub, pol = (lax.axis_index(name) for name in OWNERS)
    side, core = lax.axis_size("wide_low"), sub * pols + pol
    table = jnp.asarray(dft_table(voltages.shape[3], own * owners, wides, owners))
    table = pltpu.with_memory_space_constraint(table, pltpu.HBM)
    weights = [
        pltpu.with_memory_space_constraint(weight, pltpu.HBM)
        for weight in (real_weight, imaginary_weight)
    ]

    def numbers(*values):
        return jnp.stack(values).astype(jnp.int32)

    wide = high * side + low
    offsets = list(range(side, wides)) + list(range(side))[::-1]
    at = [wide ^ offset for offset in offsets]
    far, (volts,) = spectra(voltages, table, numbers(at[0], core), 1, subs, pols)
    near, near_kept = spectra(
        volts, table, numbers(*at[1:], core), wides - 1, subs, pols, weights, side
    )
    moved = []
    for k, piece in enumerate(far + near):
        offset = (offsets[k // subs] * subs + k % subs) * pols
        moved.append(exchange(piece, offset, OWNERS) if offset else piece)

    def both(pieces, join):
        theirs = [piece[1:] for piece in pieces]
        theirs = [jnp.concatenate(theirs)] if join else theirs
        return [*pieces, *(exchange(part, 1, ("pol",)) for part in theirs)]

    first, _ = lax.optimization_barrier((moved[:subs], near[0]))
    sums, *kept = first_beams(both(first, False), numbers(*at[:side]), weights, subs, pols)
    rest, sums = lax.optimization_barrier((moved[subs:], sums))
    total = beam_power(both(rest, True), numbers(sub), kept + near_kept, sums, wides, subs, pols)
    power = turn(total.reshape(owners, own, -1))
    return shift_and_add(power.reshape(owners * own, -1), delays, frames)


def solution(mesh):
    names = dict(zip(mesh.axis_names, mesh.devices.shape))
    low = max(1, names["wide"] // 2)
    sizes = (names["group"], names["wide"] // low, low, names["sub"], names["pol"])
    split = jax.sharding.Mesh(mesh.devices.reshape(sizes), ("group",) + OWNERS)
    placed = (
        P("pol", ("group", "wide_high", "wide_low"), "sub", None),
        P(OWNERS, None, None),
        P(OWNERS, None, None),
        P("pol", None),
    )
    return jax.shard_map(
        local,
        mesh=split,
        in_specs=placed,
        out_specs=P(("group", "wide_high", "wide_low", "sub"), None, "pol"),
        check_vma=False,
    )
```

```python
import functools
import math

import jax
import jax.numpy as jnp
import ml_dtypes
import numpy as np
from jax import lax
from jax.experimental import pallas as pl
from jax.experimental.pallas import tpu as pltpu
from jax.sharding import PartitionSpec as P

OWNERS = ("wide_high", "wide_low", "sub", "pol")
ROWS = 16
LOTS = 4
COST = pl.CostEstimate(flops=0, bytes_accessed=0, transcendentals=0)


def dft_parts(samples, channels):
    first = samples // 2 - channels
    bins = first + np.arange(channels, dtype=np.int64)
    turns = bins[:, None] * np.arange(samples, dtype=np.int64)[None, :] % samples
    angles = turns * (2.0 * math.pi / samples)
    exact = np.stack([np.cos(angles), -np.sin(angles)], axis=1) / math.sqrt(samples)
    upper = exact.astype(ml_dtypes.bfloat16)
    lower = (exact - upper.astype(np.float64)).astype(ml_dtypes.bfloat16)
    return upper, lower


def keep_weights(place_ref, first, refs, kept_refs, sem):
    copies = []
    for part, (ref, kept) in enumerate(zip(refs, kept_refs)):
        count, channels, antennas, _ = kept.shape
        lots = sem.shape[2]
        for index in range(count):
            start = pl.multiple_of(place_ref[first + index] * antennas, antennas)
            for lot in range(lots):
                some = pl.ds(lot * (channels // lots), channels // lots)
                copies.append(
                    pltpu.make_async_copy(
                        ref.at[some, pl.ds(start, antennas), :],
                        kept.at[index, some],
                        sem.at[part, index, lot],
                    )
                )
    return copies


def dft_kernel(counts, here_ref, table_ref, volt_ref, *refs):
    steps, subs, pols, parts, first = counts
    weight_refs, refs = refs[:parts], refs[parts:]
    out_refs, refs = refs[: steps * subs], refs[steps * subs :]
    kept_refs, refs = refs[:parts], refs[parts:]
    moved_ref, refs = (refs[0], refs[1:]) if first else (volt_ref, refs)
    part_ref, hold_ref, sem = refs[:3]
    frames = moved_ref.shape[0]
    copies = [
        pltpu.make_async_copy(table_ref.at[here_ref[step]], part_ref.at[step], sem.at[step])
        for step in range(steps)
    ]
    if first:
        raw_ref, raw_sem = refs[3:]
        count = raw_ref.shape[0] // raw_sem.shape[0]
        reads = []
        for index in range(raw_sem.shape[0]):
            rows = pl.ds(index * count, count)
            reads.append(
                pltpu.make_async_copy(volt_ref.at[0, rows], raw_ref.at[rows], raw_sem.at[index])
            )
        for copy in reads + copies:
            copy.start()
        for index, copy in enumerate(reads):
            copy.wait()
            rows = pl.ds(index * count, count)
            moved_ref[:, rows, :] = raw_ref[rows].transpose(1, 0, 2)
        keeps = []
    else:
        keeps = keep_weights(here_ref, steps - kept_refs[0].shape[0], weight_refs, kept_refs, refs[3])
        for copy in copies + keeps:
            copy.start()
    here = here_ref[steps]
    half = part_ref.shape[1] // 2
    for step, copy in enumerate(copies):
        copy.wait()
        for frame in range(frames):
            both = lax.dot_general(
                part_ref[step],
                moved_ref[frame],
                (((1,), (1,)), ((), ())),
                preferred_element_type=jnp.float32,
            )
            spectrum = (both[:half] + both[half:]).astype(jnp.bfloat16)
            hold_ref[step * frames + frame] = spectrum.reshape(
                subs * pols, -1, spectrum.shape[-1]
            )
            for sub in range(subs):
                for pol in range(pols):
                    out_refs[step * subs + sub][pol, frame] = hold_ref[
                        step * frames + frame, (sub * pols + pol) ^ here
                    ]
    for copy in keeps:
        copy.wait()


def spectra(volts, table, here, steps, subs, pols, weights=(), keep=0):
    first = volts.ndim == 4
    frames, antennas = volts.shape[:2] if not first else volts.shape[2:0:-1]
    samples = volts.shape[-1]
    rows = table.shape[1] // (2 * subs * pols)
    vmem = pl.BlockSpec(memory_space=pltpu.VMEM)
    hbm = pl.BlockSpec(memory_space=pltpu.HBM)
    kept = [
        pltpu.VMEM((keep, weight.shape[0], antennas, weight.shape[2]), weight.dtype)
        for weight in weights
    ]
    pieces = [jax.ShapeDtypeStruct((pols, frames, rows, antennas), jnp.bfloat16)] * (steps * subs)
    scratch = [
        pltpu.VMEM((steps,) + table.shape[1:], jnp.bfloat16),
        pltpu.VMEM((steps * frames, subs * pols, rows, antennas), jnp.bfloat16),
        pltpu.SemaphoreType.DMA((steps,)),
    ]
    if first:
        kept.append(pltpu.VMEM((frames, antennas, samples), volts.dtype))
        scratch.append(pltpu.VMEM((antennas, frames, samples), volts.dtype))
        scratch.append(pltpu.SemaphoreType.DMA((4,)))
        volts = pltpu.with_memory_space_constraint(volts, pltpu.HBM)
    else:
        scratch.append(pltpu.SemaphoreType.DMA((2, keep, LOTS)))
        volts = pltpu.with_memory_space_constraint(volts, pltpu.VMEM)
    outs = pl.pallas_call(
        functools.partial(dft_kernel, (steps, subs, pols, len(weights), first)),
        in_specs=[pl.BlockSpec(memory_space=pltpu.SMEM), hbm, hbm if first else vmem]
        + [hbm] * len(weights),
        out_specs=[vmem] * (len(pieces) + len(kept)),
        out_shape=pieces + kept,
        scratch_shapes=scratch,
        compiler_params=pltpu.CompilerParams(vmem_limit_bytes=12 * 2**20),
        name="spectra",
    )(here, table, volts, *weights)
    return list(outs[: len(pieces)]), list(outs[len(pieces) :])


def beam_rows(x_refs, index, subs, at, order_ref):
    blocks = []
    for own in (True, False):
        for piece in range(index * subs, (index + 1) * subs):
            if own:
                ref, lead = x_refs[piece], 0
            elif len(x_refs) % 2:
                ref, lead = x_refs[-1], piece
            else:
                ref, lead = x_refs[len(x_refs) // 2 + piece], 0
            frames, _, antennas = ref.shape[1:]
            block = ref[lead, :, at * ROWS : (at + 1) * ROWS, :]
            blocks.append(block.reshape(frames * ROWS, antennas))
    block = jnp.concatenate(blocks, axis=0)
    return jnp.dot(order_ref[...], block, preferred_element_type=jnp.float32).astype(jnp.bfloat16)


def beam_part(lines, half, weights):
    by_re = by_im = None
    for line, re, im in zip(lines, *weights):
        re, im = (
            jnp.dot(line, weight, preferred_element_type=jnp.float32) for weight in (re, im)
        )
        by_re = re if by_re is None else by_re + re
        by_im = im if by_im is None else by_im + im
    return by_re[:half] - by_im[half:], by_im[:half] + by_re[half:]


def antenna_lines(place_ref, index, antennas):
    return pl.ds(pl.multiple_of(place_ref[index] * antennas, antennas), antennas)


def first_kernel(subs, place_ref, order_ref, re_ref, im_ref, *refs):
    x_refs, (out_ref, re_kept, re_held, sem, kept_sem) = refs[:-5], refs[-5:]
    groups, group, antennas, _ = re_held.shape
    half = out_ref.shape[1] // 2
    own = antenna_lines(place_ref, 0, antennas)
    copies = [
        pltpu.make_async_copy(
            re_ref.at[pl.ds(at * group, group), own, :], re_held.at[at], sem.at[at]
        )
        for at in range(groups)
    ]
    keeps = keep_weights(place_ref, 1, (re_ref,), (re_kept,), kept_sem)
    for copy in copies + keeps:
        copy.start()
    for at in range(groups):
        rows = beam_rows(x_refs, 0, subs, at, order_ref)
        copies[at].wait()
        for index in range(group):
            channel = at * group + index
            line = rows[index * 2 * half : (index + 1) * 2 * half]
            weights = [re_held[at, index]], [im_ref[channel, place_ref[0]]]
            out_ref[channel, :half], out_ref[channel, half:] = beam_part([line], half, weights)
    for copy in keeps:
        copy.wait()


def last_kernel(subs, lots, place_ref, order_ref, *refs):
    kept_refs, im_ref, sum_ref, refs = refs[:lots], refs[lots], refs[lots + 1], refs[lots + 2 :]
    x_refs, (out_ref, power_ref) = refs[:-2], refs[-2:]
    re_refs = [ref.at[k] for ref in kept_refs for k in range(ref.shape[0])]
    channels, half = sum_ref.shape[0], sum_ref.shape[1] // 2
    frames = x_refs[0].shape[1]
    pols = half // (subs * frames)
    group = ROWS // 2
    owns = [place_ref[1 + k] for k in range(len(re_refs))]
    for at in range(channels // group):
        rows = [beam_rows(x_refs, k, subs, at, order_ref) for k in range(len(re_refs))]
        for index in range(group):
            channel = at * group + index
            weights = [ref[channel] for ref in re_refs], [im_ref[channel, own] for own in owns]
            lines = [row[index * 2 * half : (index + 1) * 2 * half] for row in rows]
            beam_re, beam_im = beam_part(lines, half, weights)
            beam_re = beam_re + sum_ref[channel, :half]
            beam_im = beam_im + sum_ref[channel, half:]
            power = beam_re * beam_re + beam_im * beam_im
            power = sum(power[k * subs * frames : (k + 1) * subs * frames] for k in range(pols))
            power = power - jnp.mean(power, axis=0, keepdims=True)
            for sub in range(subs):
                start = (place_ref[0] ^ sub) * frames
                for frame in range(frames):
                    power_ref[start + frame, channel] = power[sub * frames + frame]
    targets, cores = out_ref.shape[:2]
    beams = power_ref.shape[2] // targets
    for target in range(targets):
        block = jnp.concatenate(
            [power_ref[f, :, target * beams : (target + 1) * beams] for f in range(subs * frames)],
            axis=1,
        ).astype(jnp.bfloat16)
        for core in range(cores):
            out_ref[target, core] = block


def sorting(subs, pols, frames):
    group = ROWS // 2
    count = subs * pols * frames * ROWS
    spot = np.arange(count).reshape(pols, subs, frames, 2, group).transpose(4, 3, 0, 1, 2).reshape(-1)
    order = np.zeros((count, count), np.float32)
    order[np.arange(count), spot] = 1.0
    return jnp.asarray(order, jnp.bfloat16)


def first_beams(xs, place, real_weight, imaginary_weight, subs, pols):
    _, frames, _, antennas = xs[0].shape
    channels, _, beams = real_weight.shape
    group = ROWS // 2
    later = place.shape[0] - 1
    vmem = pl.BlockSpec(memory_space=pltpu.VMEM)
    hbm = pl.BlockSpec(memory_space=pltpu.HBM)
    kept = pltpu.VMEM((later, channels, antennas, beams), real_weight.dtype)
    sums = jax.ShapeDtypeStruct((channels, 2 * subs * pols * frames, beams), jnp.float32)
    return pl.pallas_call(
        functools.partial(first_kernel, subs),
        in_specs=[pl.BlockSpec(memory_space=pltpu.SMEM), vmem, hbm] + [vmem] * (1 + len(xs)),
        out_specs=[vmem] * 2,
        out_shape=[sums, kept],
        scratch_shapes=[
            pltpu.VMEM((channels // group, group, antennas, beams), real_weight.dtype),
            pltpu.SemaphoreType.DMA((channels // group,)),
            pltpu.SemaphoreType.DMA((1, later, LOTS)),
        ],
        compiler_params=pltpu.CompilerParams(vmem_limit_bytes=8 * 2**20),
        cost_estimate=pl.CostEstimate(
            flops=4 * 10**10, bytes_accessed=4 * 10**8, transcendentals=0
        ),
        name="first_beams",
    )(place, sorting(subs, pols, frames), real_weight, imaginary_weight, *xs)


def beam_power(xs, place, kept, imaginary_weight, sums, wides, subs, pols):
    frames = xs[0].shape[1]
    channels, _, beams = sums.shape
    targets = wides * subs
    width = subs * frames * (beams // targets)
    vmem = pl.BlockSpec(memory_space=pltpu.VMEM)
    return pl.pallas_call(
        functools.partial(last_kernel, subs, len(kept)),
        in_specs=[pl.BlockSpec(memory_space=pltpu.SMEM)] + [vmem] * (3 + len(kept) + len(xs)),
        out_specs=vmem,
        out_shape=jax.ShapeDtypeStruct((targets, pols, channels, width), jnp.bfloat16),
        scratch_shapes=[pltpu.VMEM((subs * frames, channels, beams), jnp.float32)],
        compiler_params=pltpu.CompilerParams(vmem_limit_bytes=4 * 2**20),
        name="beam_power",
    )(
        place,
        sorting(subs, pols, frames),
        *(pltpu.with_memory_space_constraint(part, pltpu.VMEM) for part in kept),
        imaginary_weight,
        sums,
        *xs,
    )


def exchange(x, offset, names):
    count = math.prod(lax.axis_size(name) for name in names)
    return lax.ppermute(x, names, [(k, k ^ offset) for k in range(count)])


def dft_table(samples, channels, wides, owners):
    own = channels // owners
    group = ROWS // 2

    def order(part):
        part = part.reshape(wides, owners // wides, own // group, group, 2, samples)
        return part.transpose(0, 1, 2, 4, 3, 5).reshape(wides, -1, samples)

    return np.concatenate([order(part) for part in dft_parts(samples, channels)], axis=1)


def shift_kernel(scale, power_ref, delay_ref, out_ref):
    beams, frames, _ = out_ref.shape
    delays = lax.rem(delay_ref[...], frames)
    power = power_ref[...]
    sums = [None] * frames
    for delay in range(frames):
        chosen = (delays == delay).astype(jnp.float32).astype(jnp.bfloat16)
        picked = lax.dot_general(
            power, chosen, (((0,), (1,)), ((), ())), preferred_element_type=jnp.float32
        )
        for frame in range(frames):
            row = (frame + delay) % frames * beams
            term = picked[row : row + beams]
            sums[frame] = term if sums[frame] is None else sums[frame] + term
    for frame in range(frames):
        out_ref[:, frame, :] = sums[frame] * scale


def shift_and_add(power, delays, frames):
    channels, width = power.shape
    beams = width // frames
    return pl.pallas_call(
        functools.partial(shift_kernel, 1.0 / math.sqrt(channels)),
        out_shape=jax.ShapeDtypeStruct((beams, frames, delays.shape[0]), jnp.float32),
        compiler_params=pltpu.CompilerParams(vmem_limit_bytes=8 * 2**20),
        name="shift_and_add",
    )(power, delays)


def plain_spectra(volts, owners, channels):
    frames, antennas, samples = volts.shape
    upper, lower = (jnp.asarray(part) for part in dft_parts(samples, channels))
    x = sum(
        jnp.einsum("krn,fan->kfra", part, volts, preferred_element_type=jnp.float32)
        for part in (upper, lower)
    )
    x = x.astype(jnp.bfloat16).reshape(owners, channels // owners, frames, 2, antennas)
    return x


def plain_beam_power(x, real_weight, imaginary_weight, wides, subs, pols):
    _, own, frames, _, antennas = x.shape
    beams = real_weight.shape[2]
    x = x.reshape(wides, subs, pols, own, frames, 2, antennas)
    x = x.transpose(3, 5, 2, 1, 4, 0, 6).reshape(own, 2, pols * subs * frames, wides * antennas)
    by_re, by_im = (
        jnp.einsum("crfa,cab->rcfb", x, weight, preferred_element_type=jnp.float32)
        for weight in (real_weight, imaginary_weight)
    )
    power = (by_re[0] - by_im[1]) ** 2 + (by_im[0] + by_re[1]) ** 2
    power = power.reshape(own, pols, subs * frames, beams).sum(axis=1)
    power = power - jnp.mean(power, axis=1, keepdims=True)
    targets = wides * subs
    power = power.reshape(own, subs * frames, targets, beams // targets)
    return power.transpose(2, 0, 1, 3).reshape(targets, own, -1).astype(jnp.bfloat16)


def plain_shift_and_add(power, delays, frames):
    channels = power.shape[0]
    power = power.reshape(channels, frames, -1)
    chosen = (delays[None] % frames == jnp.arange(frames)[:, None, None]).astype(jnp.bfloat16)
    picked = jnp.einsum("dtc,cfb->dbft", chosen, power, preferred_element_type=jnp.float32)
    moved = sum(jnp.roll(picked[delay], -delay, axis=1) for delay in range(frames))
    return moved * (1.0 / math.sqrt(channels))


def local(voltages, real_weight, imaginary_weight, delays):
    highs, lows, subs, pols = (lax.axis_size(name) for name in OWNERS)
    wides = highs * lows
    owners = wides * subs * pols
    own, _, beams = real_weight.shape
    frames = subs * voltages.shape[2]
    tiled = (
        own % ROWS == 0
        and voltages.shape[1] % 128 == 0
        and (beams // (wides * subs)) % 32 == 0
        and frames == 4
        and (wides, subs, pols) == (4, 2, 2)
    )
    turn = functools.partial(
        lax.all_to_all, axis_name=OWNERS, split_axis=0, concat_axis=0, tiled=True
    )
    if not tiled:
        volts = jnp.transpose(voltages[0], (1, 0, 2))
        x = turn(plain_spectra(volts, owners, own * owners))
        power = plain_beam_power(x, real_weight, imaginary_weight, wides, subs, pols)
        power = jnp.broadcast_to(power[:, None], (wides * subs, pols) + power.shape[1:])
        power = turn(power.reshape(owners, own, -1))
        return plain_shift_and_add(power.reshape(owners * own, -1), delays, frames)
    high, low, sub, pol = (lax.axis_index(name) for name in OWNERS)
    side, core = lax.axis_size("wide_low"), sub * pols + pol
    table = jnp.asarray(dft_table(voltages.shape[3], own * owners, wides, owners))
    table = pltpu.with_memory_space_constraint(table, pltpu.HBM)
    real_weight = pltpu.with_memory_space_constraint(real_weight, pltpu.HBM)

    def numbers(*values):
        return jnp.stack(values).astype(jnp.int32)

    wide = high * side + low
    offsets = list(range(side, wides)) + list(range(side))[::-1]
    at = [wide ^ offset for offset in offsets]
    far, (volts,) = spectra(voltages, table, numbers(at[0], core), 1, subs, pols)
    imaginary_weight = imaginary_weight.reshape(own, wides, -1, beams)
    imaginary_weight, _ = lax.optimization_barrier((imaginary_weight, far[0]))
    imaginary_weight = pltpu.with_memory_space_constraint(imaginary_weight, pltpu.VMEM)
    near, near_kept = spectra(
        volts, table, numbers(*at[1:], core), wides - 1, subs, pols, [real_weight], side
    )
    moved = []
    for k, piece in enumerate(far + near):
        offset = (offsets[k // subs] * subs + k % subs) * pols
        moved.append(exchange(piece, offset, OWNERS) if offset else piece)

    def both(pieces, join):
        theirs = [piece[1:] for piece in pieces]
        theirs = [jnp.concatenate(theirs)] if join else theirs
        return [*pieces, *(exchange(part, 1, ("pol",)) for part in theirs)]

    first, _ = lax.optimization_barrier((moved[:subs], near[0]))
    sums, kept = first_beams(
        both(first, False), numbers(*at[:side]), real_weight, imaginary_weight, subs, pols
    )
    rest = moved[subs:]
    longest = rest.pop(2 * subs - 1)
    longest, rest, sums = lax.optimization_barrier((longest, rest, sums))
    rest.insert(2 * subs - 1, longest)
    total = beam_power(
        both(rest, True),
        numbers(sub, *at[1:]),
        [kept] + near_kept,
        imaginary_weight,
        sums,
        wides,
        subs,
        pols,
    )
    power = turn(total.reshape(owners, own, -1))
    return shift_and_add(power.reshape(owners * own, -1), delays, frames)


def solution(mesh):
    names = dict(zip(mesh.axis_names, mesh.devices.shape))
    low = max(1, names["wide"] // 2)
    sizes = (names["group"], names["wide"] // low, low, names["sub"], names["pol"])
    split = jax.sharding.Mesh(mesh.devices.reshape(sizes), ("group",) + OWNERS)
    placed = (
        P("pol", ("group", "wide_high", "wide_low"), "sub", None),
        P(OWNERS, None, None),
        P(OWNERS, None, None),
        P("pol", None),
    )
    return jax.shard_map(
        local,
        mesh=split,
        in_specs=placed,
        out_specs=P(("group", "wide_high", "wide_low", "sub"), None, "pol"),
        check_vma=False,
    )
```

```python
import functools
import math

import jax
import jax.numpy as jnp
import ml_dtypes
import numpy as np
from jax import lax
from jax.experimental import pallas as pl
from jax.experimental.pallas import tpu as pltpu
from jax.sharding import PartitionSpec as P

OWNERS = ("wide_high", "wide_low", "sub", "pol")
ROWS = 16
LOTS = 4
PARTS = 4
COST = pl.CostEstimate(flops=0, bytes_accessed=0, transcendentals=0)


def dft_parts(samples, channels):
    first = samples // 2 - channels
    bins = first + np.arange(channels, dtype=np.int64)
    turns = bins[:, None] * np.arange(samples, dtype=np.int64)[None, :] % samples
    angles = turns * (2.0 * math.pi / samples)
    exact = np.stack([np.cos(angles), -np.sin(angles)], axis=1) / math.sqrt(samples)
    upper = exact.astype(ml_dtypes.bfloat16)
    lower = (exact - upper.astype(np.float64)).astype(ml_dtypes.bfloat16)
    return upper, lower


def keep_weights(place_ref, first, refs, kept_refs, sem):
    copies = []
    for part, (ref, kept) in enumerate(zip(refs, kept_refs)):
        count, channels, antennas, _ = kept.shape
        lots = sem.shape[2]
        for index in range(count):
            start = pl.multiple_of(place_ref[first + index] * antennas, antennas)
            for lot in range(lots):
                some = pl.ds(lot * (channels // lots), channels // lots)
                copies.append(
                    pltpu.make_async_copy(
                        ref.at[some, pl.ds(start, antennas), :],
                        kept.at[index, some],
                        sem.at[part, index, lot],
                    )
                )
    return copies


def dft_kernel(counts, here_ref, table_ref, volt_ref, *refs):
    steps, subs, pols, parts, first = counts
    weight_refs, refs = refs[:parts], refs[parts:]
    out_refs, refs = refs[: steps * subs], refs[steps * subs :]
    kept_refs, refs = refs[:parts], refs[parts:]
    moved_ref, refs = (refs[0], refs[1:]) if first else (volt_ref, refs)
    part_ref, hold_ref, sem = refs[:3]
    frames = moved_ref.shape[0]
    here = here_ref[steps]

    def give(step, frame, both):
        half = both.shape[0] // 2
        spectrum = (both[:half] + both[half:]).astype(jnp.bfloat16)
        hold_ref[step * frames + frame] = spectrum.reshape(subs * pols, -1, spectrum.shape[-1])
        for sub in range(subs):
            for pol in range(pols):
                out_refs[step * subs + sub][pol, frame] = hold_ref[
                    step * frames + frame, (sub * pols + pol) ^ here
                ]

    def product(part, volts):
        return lax.dot_general(
            part, volts, (((1,), (1,)), ((), ())), preferred_element_type=jnp.float32
        )

    if first:
        raw_ref, raw_sem = refs[3:]
        lots, _, _, width = raw_ref.shape
        copies = []
        for lot in range(lots):
            some = pl.ds(lot * width, width)
            copies.append(
                (
                    pltpu.make_async_copy(
                        volt_ref.at[0, :, :, some], raw_ref.at[lot], raw_sem.at[0, lot]
                    ),
                    pltpu.make_async_copy(
                        table_ref.at[here_ref[0], :, some], part_ref.at[lot], raw_sem.at[1, lot]
                    ),
                )
            )
        for pair in copies:
            for copy in pair:
                copy.start()
        sums = [None] * frames
        for lot, (read, part) in enumerate(copies):
            some = pl.ds(lot * width, width)
            read.wait()
            moved_ref[:, :, some] = raw_ref[lot].transpose(1, 0, 2)
            part.wait()
            for frame in range(frames):
                term = product(part_ref[lot], moved_ref[frame, :, some])
                sums[frame] = term if lot == 0 else sums[frame] + term
        for frame in range(frames):
            give(0, frame, sums[frame])
        return
    copies = [
        pltpu.make_async_copy(table_ref.at[here_ref[step]], part_ref.at[step], sem.at[step])
        for step in range(steps)
    ]
    keeps = keep_weights(here_ref, steps - kept_refs[0].shape[0], weight_refs, kept_refs, refs[3])
    for copy in copies + keeps:
        copy.start()
    for step, copy in enumerate(copies):
        copy.wait()
        for frame in range(frames):
            give(step, frame, product(part_ref[step], moved_ref[frame]))
    for copy in keeps:
        copy.wait()


def spectra(volts, table, here, steps, subs, pols, weights=(), keep=0):
    first = volts.ndim == 4
    frames, antennas = volts.shape[:2] if not first else volts.shape[2:0:-1]
    samples = volts.shape[-1]
    rows = table.shape[1] // (2 * subs * pols)
    vmem = pl.BlockSpec(memory_space=pltpu.VMEM)
    hbm = pl.BlockSpec(memory_space=pltpu.HBM)
    kept = [
        pltpu.VMEM((keep, weight.shape[0], antennas, weight.shape[2]), weight.dtype)
        for weight in weights
    ]
    pieces = [jax.ShapeDtypeStruct((pols, frames, rows, antennas), jnp.bfloat16)] * (steps * subs)
    part = (steps,) + table.shape[1:]
    if first:
        part = (PARTS, table.shape[1], samples // PARTS)
    scratch = [
        pltpu.VMEM(part, jnp.bfloat16),
        pltpu.VMEM((steps * frames, subs * pols, rows, antennas), jnp.bfloat16),
        pltpu.SemaphoreType.DMA((steps,)),
    ]
    if first:
        kept.append(pltpu.VMEM((frames, antennas, samples), volts.dtype))
        scratch.append(pltpu.VMEM((PARTS, antennas, frames, samples // PARTS), volts.dtype))
        scratch.append(pltpu.SemaphoreType.DMA((2, PARTS)))
        volts = pltpu.with_memory_space_constraint(volts, pltpu.HBM)
    else:
        scratch.append(pltpu.SemaphoreType.DMA((2, keep, LOTS)))
        volts = pltpu.with_memory_space_constraint(volts, pltpu.VMEM)
    outs = pl.pallas_call(
        functools.partial(dft_kernel, (steps, subs, pols, len(weights), first)),
        in_specs=[pl.BlockSpec(memory_space=pltpu.SMEM), hbm, hbm if first else vmem]
        + [hbm] * len(weights),
        out_specs=[vmem] * (len(pieces) + len(kept)),
        out_shape=pieces + kept,
        scratch_shapes=scratch,
        compiler_params=pltpu.CompilerParams(vmem_limit_bytes=12 * 2**20),
        name="spectra",
    )(here, table, volts, *weights)
    return list(outs[: len(pieces)]), list(outs[len(pieces) :])


def beam_rows(x_refs, index, subs, at, order_ref):
    blocks = []
    for own in (True, False):
        for piece in range(index * subs, (index + 1) * subs):
            if own:
                ref, lead = x_refs[piece], 0
            elif len(x_refs) % 2:
                ref, lead = x_refs[-1], piece
            else:
                ref, lead = x_refs[len(x_refs) // 2 + piece], 0
            frames, _, antennas = ref.shape[1:]
            block = ref[lead, :, at * ROWS : (at + 1) * ROWS, :]
            blocks.append(block.reshape(frames * ROWS, antennas))
    block = jnp.concatenate(blocks, axis=0)
    return jnp.dot(order_ref[...], block, preferred_element_type=jnp.float32).astype(jnp.bfloat16)


def beam_part(lines, half, weights):
    by_re = by_im = None
    for line, re, im in zip(lines, *weights):
        re, im = (
            jnp.dot(line, weight, preferred_element_type=jnp.float32) for weight in (re, im)
        )
        by_re = re if by_re is None else by_re + re
        by_im = im if by_im is None else by_im + im
    return by_re[:half] - by_im[half:], by_im[:half] + by_re[half:]


def antenna_lines(place_ref, index, antennas):
    return pl.ds(pl.multiple_of(place_ref[index] * antennas, antennas), antennas)


def first_kernel(subs, place_ref, order_ref, re_ref, im_ref, *refs):
    x_refs, (out_ref, re_kept, re_held, sem, kept_sem) = refs[:-5], refs[-5:]
    groups, group, antennas, _ = re_held.shape
    half = out_ref.shape[1] // 2
    own = antenna_lines(place_ref, 0, antennas)
    copies = [
        pltpu.make_async_copy(
            re_ref.at[pl.ds(at * group, group), own, :], re_held.at[at], sem.at[at]
        )
        for at in range(groups)
    ]
    keeps = keep_weights(place_ref, 1, (re_ref,), (re_kept,), kept_sem)
    for copy in copies + keeps:
        copy.start()
    for at in range(groups):
        rows = beam_rows(x_refs, 0, subs, at, order_ref)
        copies[at].wait()
        for index in range(group):
            channel = at * group + index
            line = rows[index * 2 * half : (index + 1) * 2 * half]
            weights = [re_held[at, index]], [im_ref[channel, place_ref[0]]]
            out_ref[channel, :half], out_ref[channel, half:] = beam_part([line], half, weights)
    for copy in keeps:
        copy.wait()


def last_kernel(subs, lots, place_ref, order_ref, *refs):
    kept_refs, im_ref, sum_ref, refs = refs[:lots], refs[lots], refs[lots + 1], refs[lots + 2 :]
    x_refs, (out_ref, power_ref) = refs[:-2], refs[-2:]
    re_refs = [ref.at[k] for ref in kept_refs for k in range(ref.shape[0])]
    channels, half = sum_ref.shape[0], sum_ref.shape[1] // 2
    frames = x_refs[0].shape[1]
    pols = half // (subs * frames)
    group = ROWS // 2
    owns = [place_ref[1 + k] for k in range(len(re_refs))]
    for at in range(channels // group):
        rows = [beam_rows(x_refs, k, subs, at, order_ref) for k in range(len(re_refs))]
        for index in range(group):
            channel = at * group + index
            weights = [ref[channel] for ref in re_refs], [im_ref[channel, own] for own in owns]
            lines = [row[index * 2 * half : (index + 1) * 2 * half] for row in rows]
            beam_re, beam_im = beam_part(lines, half, weights)
            beam_re = beam_re + sum_ref[channel, :half]
            beam_im = beam_im + sum_ref[channel, half:]
            power = beam_re * beam_re + beam_im * beam_im
            power = sum(power[k * subs * frames : (k + 1) * subs * frames] for k in range(pols))
            power = power - jnp.mean(power, axis=0, keepdims=True)
            for sub in range(subs):
                start = (place_ref[0] ^ sub) * frames
                for frame in range(frames):
                    power_ref[start + frame, channel] = power[sub * frames + frame]
    targets, cores = out_ref.shape[:2]
    beams = power_ref.shape[2] // targets
    for target in range(targets):
        block = jnp.concatenate(
            [power_ref[f, :, target * beams : (target + 1) * beams] for f in range(subs * frames)],
            axis=1,
        ).astype(jnp.bfloat16)
        for core in range(cores):
            out_ref[target, core] = block


def sorting(subs, pols, frames):
    group = ROWS // 2
    count = subs * pols * frames * ROWS
    spot = np.arange(count).reshape(pols, subs, frames, 2, group).transpose(4, 3, 0, 1, 2).reshape(-1)
    order = np.zeros((count, count), np.float32)
    order[np.arange(count), spot] = 1.0
    return jnp.asarray(order, jnp.bfloat16)


def first_beams(xs, place, real_weight, imaginary_weight, subs, pols):
    _, frames, _, antennas = xs[0].shape
    channels, _, beams = real_weight.shape
    group = ROWS // 2
    later = place.shape[0] - 1
    vmem = pl.BlockSpec(memory_space=pltpu.VMEM)
    hbm = pl.BlockSpec(memory_space=pltpu.HBM)
    kept = pltpu.VMEM((later, channels, antennas, beams), real_weight.dtype)
    sums = jax.ShapeDtypeStruct((channels, 2 * subs * pols * frames, beams), jnp.float32)
    return pl.pallas_call(
        functools.partial(first_kernel, subs),
        in_specs=[pl.BlockSpec(memory_space=pltpu.SMEM), vmem, hbm] + [vmem] * (1 + len(xs)),
        out_specs=[vmem] * 2,
        out_shape=[sums, kept],
        scratch_shapes=[
            pltpu.VMEM((channels // group, group, antennas, beams), real_weight.dtype),
            pltpu.SemaphoreType.DMA((channels // group,)),
            pltpu.SemaphoreType.DMA((1, later, LOTS)),
        ],
        compiler_params=pltpu.CompilerParams(vmem_limit_bytes=8 * 2**20),
        cost_estimate=pl.CostEstimate(
            flops=4 * 10**10, bytes_accessed=4 * 10**8, transcendentals=0
        ),
        name="first_beams",
    )(place, sorting(subs, pols, frames), real_weight, imaginary_weight, *xs)


def beam_power(xs, place, kept, imaginary_weight, sums, wides, subs, pols):
    frames = xs[0].shape[1]
    channels, _, beams = sums.shape
    targets = wides * subs
    width = subs * frames * (beams // targets)
    vmem = pl.BlockSpec(memory_space=pltpu.VMEM)
    return pl.pallas_call(
        functools.partial(last_kernel, subs, len(kept)),
        in_specs=[pl.BlockSpec(memory_space=pltpu.SMEM)] + [vmem] * (3 + len(kept) + len(xs)),
        out_specs=vmem,
        out_shape=jax.ShapeDtypeStruct((targets, pols, channels, width), jnp.bfloat16),
        scratch_shapes=[pltpu.VMEM((subs * frames, channels, beams), jnp.float32)],
        compiler_params=pltpu.CompilerParams(vmem_limit_bytes=4 * 2**20),
        name="beam_power",
    )(
        place,
        sorting(subs, pols, frames),
        *(pltpu.with_memory_space_constraint(part, pltpu.VMEM) for part in kept),
        imaginary_weight,
        sums,
        *xs,
    )


def exchange(x, offset, names):
    count = math.prod(lax.axis_size(name) for name in names)
    return lax.ppermute(x, names, [(k, k ^ offset) for k in range(count)])


def dft_table(samples, channels, wides, owners):
    own = channels // owners
    group = ROWS // 2

    def order(part):
        part = part.reshape(wides, owners // wides, own // group, group, 2, samples)
        return part.transpose(0, 1, 2, 4, 3, 5).reshape(wides, -1, samples)

    return np.concatenate([order(part) for part in dft_parts(samples, channels)], axis=1)


def shift_kernel(scale, power_ref, delay_ref, out_ref):
    beams, frames, _ = out_ref.shape
    delays = lax.rem(delay_ref[...], frames)
    power = power_ref[...]
    sums = [None] * frames
    for delay in range(frames):
        chosen = (delays == delay).astype(jnp.float32).astype(jnp.bfloat16)
        picked = lax.dot_general(
            power, chosen, (((0,), (1,)), ((), ())), preferred_element_type=jnp.float32
        )
        for frame in range(frames):
            row = (frame + delay) % frames * beams
            term = picked[row : row + beams]
            sums[frame] = term if sums[frame] is None else sums[frame] + term
    for frame in range(frames):
        out_ref[:, frame, :] = sums[frame] * scale


def shift_and_add(power, delays, frames):
    channels, width = power.shape
    beams = width // frames
    return pl.pallas_call(
        functools.partial(shift_kernel, 1.0 / math.sqrt(channels)),
        out_shape=jax.ShapeDtypeStruct((beams, frames, delays.shape[0]), jnp.float32),
        compiler_params=pltpu.CompilerParams(vmem_limit_bytes=8 * 2**20),
        name="shift_and_add",
    )(power, delays)


def plain_spectra(volts, owners, channels):
    frames, antennas, samples = volts.shape
    upper, lower = (jnp.asarray(part) for part in dft_parts(samples, channels))
    x = sum(
        jnp.einsum("krn,fan->kfra", part, volts, preferred_element_type=jnp.float32)
        for part in (upper, lower)
    )
    x = x.astype(jnp.bfloat16).reshape(owners, channels // owners, frames, 2, antennas)
    return x


def plain_beam_power(x, real_weight, imaginary_weight, wides, subs, pols):
    _, own, frames, _, antennas = x.shape
    beams = real_weight.shape[2]
    x = x.reshape(wides, subs, pols, own, frames, 2, antennas)
    x = x.transpose(3, 5, 2, 1, 4, 0, 6).reshape(own, 2, pols * subs * frames, wides * antennas)
    by_re, by_im = (
        jnp.einsum("crfa,cab->rcfb", x, weight, preferred_element_type=jnp.float32)
        for weight in (real_weight, imaginary_weight)
    )
    power = (by_re[0] - by_im[1]) ** 2 + (by_im[0] + by_re[1]) ** 2
    power = power.reshape(own, pols, subs * frames, beams).sum(axis=1)
    power = power - jnp.mean(power, axis=1, keepdims=True)
    targets = wides * subs
    power = power.reshape(own, subs * frames, targets, beams // targets)
    return power.transpose(2, 0, 1, 3).reshape(targets, own, -1).astype(jnp.bfloat16)


def plain_shift_and_add(power, delays, frames):
    channels = power.shape[0]
    power = power.reshape(channels, frames, -1)
    chosen = (delays[None] % frames == jnp.arange(frames)[:, None, None]).astype(jnp.bfloat16)
    picked = jnp.einsum("dtc,cfb->dbft", chosen, power, preferred_element_type=jnp.float32)
    moved = sum(jnp.roll(picked[delay], -delay, axis=1) for delay in range(frames))
    return moved * (1.0 / math.sqrt(channels))


def local(voltages, real_weight, imaginary_weight, delays):
    highs, lows, subs, pols = (lax.axis_size(name) for name in OWNERS)
    wides = highs * lows
    owners = wides * subs * pols
    own, _, beams = real_weight.shape
    frames = subs * voltages.shape[2]
    tiled = (
        own % ROWS == 0
        and voltages.shape[1] % 128 == 0
        and (beams // (wides * subs)) % 32 == 0
        and frames == 4
        and (wides, subs, pols) == (4, 2, 2)
    )
    turn = functools.partial(
        lax.all_to_all, axis_name=OWNERS, split_axis=0, concat_axis=0, tiled=True
    )
    if not tiled:
        volts = jnp.transpose(voltages[0], (1, 0, 2))
        x = turn(plain_spectra(volts, owners, own * owners))
        power = plain_beam_power(x, real_weight, imaginary_weight, wides, subs, pols)
        power = jnp.broadcast_to(power[:, None], (wides * subs, pols) + power.shape[1:])
        power = turn(power.reshape(owners, own, -1))
        return plain_shift_and_add(power.reshape(owners * own, -1), delays, frames)
    high, low, sub, pol = (lax.axis_index(name) for name in OWNERS)
    side, core = lax.axis_size("wide_low"), sub * pols + pol
    table = jnp.asarray(dft_table(voltages.shape[3], own * owners, wides, owners))
    table = pltpu.with_memory_space_constraint(table, pltpu.HBM)
    real_weight = pltpu.with_memory_space_constraint(real_weight, pltpu.HBM)

    def numbers(*values):
        return jnp.stack(values).astype(jnp.int32)

    wide = high * side + low
    offsets = list(range(side, wides)) + list(range(side))[::-1]
    at = [wide ^ offset for offset in offsets]
    far, (volts,) = spectra(voltages, table, numbers(at[0], core), 1, subs, pols)
    imaginary_weight = imaginary_weight.reshape(own, wides, -1, beams)
    imaginary_weight, _ = lax.optimization_barrier((imaginary_weight, far[0]))
    imaginary_weight = pltpu.with_memory_space_constraint(imaginary_weight, pltpu.VMEM)
    near, near_kept = spectra(
        volts, table, numbers(*at[1:], core), wides - 1, subs, pols, [real_weight], side
    )
    moved = []
    for k, piece in enumerate(far + near):
        offset = (offsets[k // subs] * subs + k % subs) * pols
        moved.append(exchange(piece, offset, OWNERS) if offset else piece)

    def both(pieces, join):
        theirs = [piece[1:] for piece in pieces]
        theirs = [jnp.concatenate(theirs)] if join else theirs
        return [*pieces, *(exchange(part, 1, ("pol",)) for part in theirs)]

    first, _ = lax.optimization_barrier((moved[:subs], near[0]))
    sums, kept = first_beams(
        both(first, False), numbers(*at[:side]), real_weight, imaginary_weight, subs, pols
    )
    rest = moved[subs:]
    longest = rest.pop(2 * subs - 1)
    longest, rest, sums = lax.optimization_barrier((longest, rest, sums))
    rest.insert(2 * subs - 1, longest)
    total = beam_power(
        both(rest, True),
        numbers(sub, *at[1:]),
        [kept] + near_kept,
        imaginary_weight,
        sums,
        wides,
        subs,
        pols,
    )
    power = turn(total.reshape(owners, own, -1))
    return shift_and_add(power.reshape(owners * own, -1), delays, frames)


def solution(mesh):
    names = dict(zip(mesh.axis_names, mesh.devices.shape))
    low = max(1, names["wide"] // 2)
    sizes = (names["group"], names["wide"] // low, low, names["sub"], names["pol"])
    split = jax.sharding.Mesh(mesh.devices.reshape(sizes), ("group",) + OWNERS)
    placed = (
        P("pol", ("group", "wide_high", "wide_low"), "sub", None),
        P(OWNERS, None, None),
        P(OWNERS, None, None),
        P("pol", None),
    )
    return jax.shard_map(
        local,
        mesh=split,
        in_specs=placed,
        out_specs=P(("group", "wide_high", "wide_low", "sub"), None, "pol"),
        check_vma=False,
    )
```

```python
import functools
import math

import jax
import jax.numpy as jnp
import ml_dtypes
import numpy as np
from jax import lax
from jax.experimental import pallas as pl
from jax.experimental.pallas import tpu as pltpu
from jax.sharding import PartitionSpec as P

OWNERS = ("wide_high", "wide_low", "sub", "pol")
ROWS = 16
LOTS = 4
PARTS = 8
COST = pl.CostEstimate(flops=0, bytes_accessed=0, transcendentals=0)


def dft_parts(samples, channels):
    first = samples // 2 - channels
    bins = first + np.arange(channels, dtype=np.int64)
    turns = bins[:, None] * np.arange(samples, dtype=np.int64)[None, :] % samples
    angles = turns * (2.0 * math.pi / samples)
    exact = np.stack([np.cos(angles), -np.sin(angles)], axis=1) / math.sqrt(samples)
    upper = exact.astype(ml_dtypes.bfloat16)
    lower = (exact - upper.astype(np.float64)).astype(ml_dtypes.bfloat16)
    return upper, lower


def keep_weights(place_ref, first, refs, kept_refs, sem):
    copies = []
    for part, (ref, kept) in enumerate(zip(refs, kept_refs)):
        count, channels, antennas, _ = kept.shape
        lots = sem.shape[2]
        for index in range(count):
            start = pl.multiple_of(place_ref[first + index] * antennas, antennas)
            for lot in range(lots):
                some = pl.ds(lot * (channels // lots), channels // lots)
                copies.append(
                    pltpu.make_async_copy(
                        ref.at[some, pl.ds(start, antennas), :],
                        kept.at[index, some],
                        sem.at[part, index, lot],
                    )
                )
    return copies


def dft_kernel(counts, here_ref, table_ref, volt_ref, *refs):
    steps, subs, pols, parts, first = counts
    weight_refs, refs = refs[:parts], refs[parts:]
    out_refs, refs = refs[: steps * subs], refs[steps * subs :]
    kept_refs, refs = refs[:parts], refs[parts:]
    moved_ref, refs = (refs[0], refs[1:]) if first else (volt_ref, refs)
    part_ref, hold_ref, sem = refs[:3]
    frames = moved_ref.shape[0]
    here = here_ref[steps]

    def give(step, frame, both):
        half = both.shape[0] // 2
        spectrum = (both[:half] + both[half:]).astype(jnp.bfloat16)
        hold_ref[step * frames + frame] = spectrum.reshape(subs * pols, -1, spectrum.shape[-1])
        for sub in range(subs):
            for pol in range(pols):
                out_refs[step * subs + sub][pol, frame] = hold_ref[
                    step * frames + frame, (sub * pols + pol) ^ here
                ]

    def product(part, volts):
        return lax.dot_general(
            part, volts, (((1,), (1,)), ((), ())), preferred_element_type=jnp.float32
        )

    if first:
        raw_ref, raw_sem = refs[3:]
        lots, _, _, width = raw_ref.shape
        copies = []
        for lot in range(lots):
            some = pl.ds(lot * width, width)
            copies.append(
                (
                    pltpu.make_async_copy(
                        volt_ref.at[0, :, :, some], raw_ref.at[lot], raw_sem.at[0, lot]
                    ),
                    pltpu.make_async_copy(
                        table_ref.at[here_ref[0], :, some], part_ref.at[lot], raw_sem.at[1, lot]
                    ),
                )
            )
        for pair in copies:
            for copy in pair:
                copy.start()
        sums = [None] * frames
        for lot, (read, part) in enumerate(copies):
            some = pl.ds(lot * width, width)
            read.wait()
            moved_ref[:, :, some] = raw_ref[lot].transpose(1, 0, 2)
            part.wait()
            for frame in range(frames):
                term = product(part_ref[lot], moved_ref[frame, :, some])
                sums[frame] = term if lot == 0 else sums[frame] + term
        for frame in range(frames):
            give(0, frame, sums[frame])
        return
    copies = [
        pltpu.make_async_copy(table_ref.at[here_ref[step]], part_ref.at[step], sem.at[step])
        for step in range(steps)
    ]
    keeps = keep_weights(here_ref, steps - kept_refs[0].shape[0], weight_refs, kept_refs, refs[3])
    for copy in copies + keeps:
        copy.start()
    for step, copy in enumerate(copies):
        copy.wait()
        for frame in range(frames):
            give(step, frame, product(part_ref[step], moved_ref[frame]))
    for copy in keeps:
        copy.wait()


def spectra(volts, table, here, steps, subs, pols, weights=(), keep=0):
    first = volts.ndim == 4
    frames, antennas = volts.shape[:2] if not first else volts.shape[2:0:-1]
    samples = volts.shape[-1]
    rows = table.shape[1] // (2 * subs * pols)
    vmem = pl.BlockSpec(memory_space=pltpu.VMEM)
    hbm = pl.BlockSpec(memory_space=pltpu.HBM)
    kept = [
        pltpu.VMEM((keep, weight.shape[0], antennas, weight.shape[2]), weight.dtype)
        for weight in weights
    ]
    pieces = [jax.ShapeDtypeStruct((pols, frames, rows, antennas), jnp.bfloat16)] * (steps * subs)
    part = (steps,) + table.shape[1:]
    if first:
        part = (PARTS, table.shape[1], samples // PARTS)
    scratch = [
        pltpu.VMEM(part, jnp.bfloat16),
        pltpu.VMEM((steps * frames, subs * pols, rows, antennas), jnp.bfloat16),
        pltpu.SemaphoreType.DMA((steps,)),
    ]
    if first:
        kept.append(pltpu.VMEM((frames, antennas, samples), volts.dtype))
        scratch.append(pltpu.VMEM((PARTS, antennas, frames, samples // PARTS), volts.dtype))
        scratch.append(pltpu.SemaphoreType.DMA((2, PARTS)))
        volts = pltpu.with_memory_space_constraint(volts, pltpu.HBM)
    else:
        scratch.append(pltpu.SemaphoreType.DMA((2, keep, LOTS)))
        volts = pltpu.with_memory_space_constraint(volts, pltpu.VMEM)
    outs = pl.pallas_call(
        functools.partial(dft_kernel, (steps, subs, pols, len(weights), first)),
        in_specs=[pl.BlockSpec(memory_space=pltpu.SMEM), hbm, hbm if first else vmem]
        + [hbm] * len(weights),
        out_specs=[vmem] * (len(pieces) + len(kept)),
        out_shape=pieces + kept,
        scratch_shapes=scratch,
        compiler_params=pltpu.CompilerParams(vmem_limit_bytes=12 * 2**20),
        name="spectra",
    )(here, table, volts, *weights)
    return list(outs[: len(pieces)]), list(outs[len(pieces) :])


def beam_rows(x_refs, index, subs, at, order_ref):
    blocks = []
    for own in (True, False):
        for piece in range(index * subs, (index + 1) * subs):
            if own:
                ref, lead = x_refs[piece], 0
            elif len(x_refs) % 2:
                ref, lead = x_refs[-1], piece
            else:
                ref, lead = x_refs[len(x_refs) // 2 + piece], 0
            frames, _, antennas = ref.shape[1:]
            block = ref[lead, :, at * ROWS : (at + 1) * ROWS, :]
            blocks.append(block.reshape(frames * ROWS, antennas))
    block = jnp.concatenate(blocks, axis=0)
    return jnp.dot(order_ref[...], block, preferred_element_type=jnp.float32).astype(jnp.bfloat16)


def beam_part(lines, half, weights):
    by_re = by_im = None
    for line, re, im in zip(lines, *weights):
        re, im = (
            jnp.dot(line, weight, preferred_element_type=jnp.float32) for weight in (re, im)
        )
        by_re = re if by_re is None else by_re + re
        by_im = im if by_im is None else by_im + im
    return by_re[:half] - by_im[half:], by_im[:half] + by_re[half:]


def antenna_lines(place_ref, index, antennas):
    return pl.ds(pl.multiple_of(place_ref[index] * antennas, antennas), antennas)


def first_kernel(subs, place_ref, order_ref, re_ref, im_ref, *refs):
    x_refs, (out_ref, re_kept, re_held, sem, kept_sem) = refs[:-5], refs[-5:]
    groups, group, antennas, _ = re_held.shape
    half = out_ref.shape[1] // 2
    own = antenna_lines(place_ref, 0, antennas)
    copies = [
        pltpu.make_async_copy(
            re_ref.at[pl.ds(at * group, group), own, :], re_held.at[at], sem.at[at]
        )
        for at in range(groups)
    ]
    keeps = keep_weights(place_ref, 1, (re_ref,), (re_kept,), kept_sem)
    for copy in copies + keeps:
        copy.start()
    for at in range(groups):
        rows = beam_rows(x_refs, 0, subs, at, order_ref)
        copies[at].wait()
        for index in range(group):
            channel = at * group + index
            line = rows[index * 2 * half : (index + 1) * 2 * half]
            weights = [re_held[at, index]], [im_ref[channel, place_ref[0]]]
            out_ref[channel, :half], out_ref[channel, half:] = beam_part([line], half, weights)
    for copy in keeps:
        copy.wait()


def last_kernel(subs, lots, place_ref, order_ref, *refs):
    kept_refs, im_ref, sum_ref, refs = refs[:lots], refs[lots], refs[lots + 1], refs[lots + 2 :]
    x_refs, (out_ref, power_ref) = refs[:-2], refs[-2:]
    re_refs = [ref.at[k] for ref in kept_refs for k in range(ref.shape[0])]
    channels, half = sum_ref.shape[0], sum_ref.shape[1] // 2
    frames = x_refs[0].shape[1]
    pols = half // (subs * frames)
    group = ROWS // 2
    owns = [place_ref[1 + k] for k in range(len(re_refs))]
    for at in range(channels // group):
        rows = [beam_rows(x_refs, k, subs, at, order_ref) for k in range(len(re_refs))]
        for index in range(group):
            channel = at * group + index
            weights = [ref[channel] for ref in re_refs], [im_ref[channel, own] for own in owns]
            lines = [row[index * 2 * half : (index + 1) * 2 * half] for row in rows]
            beam_re, beam_im = beam_part(lines, half, weights)
            beam_re = beam_re + sum_ref[channel, :half]
            beam_im = beam_im + sum_ref[channel, half:]
            power = beam_re * beam_re + beam_im * beam_im
            power = sum(power[k * subs * frames : (k + 1) * subs * frames] for k in range(pols))
            power = power - jnp.mean(power, axis=0, keepdims=True)
            for sub in range(subs):
                start = (place_ref[0] ^ sub) * frames
                for frame in range(frames):
                    power_ref[start + frame, channel] = power[sub * frames + frame]
    targets, cores = out_ref.shape[:2]
    beams = power_ref.shape[2] // targets
    for target in range(targets):
        block = jnp.concatenate(
            [power_ref[f, :, target * beams : (target + 1) * beams] for f in range(subs * frames)],
            axis=1,
        ).astype(jnp.bfloat16)
        for core in range(cores):
            out_ref[target, core] = block


def sorting(subs, pols, frames):
    group = ROWS // 2
    count = subs * pols * frames * ROWS
    spot = np.arange(count).reshape(pols, subs, frames, 2, group).transpose(4, 3, 0, 1, 2).reshape(-1)
    order = np.zeros((count, count), np.float32)
    order[np.arange(count), spot] = 1.0
    return jnp.asarray(order, jnp.bfloat16)


def first_beams(xs, place, real_weight, imaginary_weight, subs, pols):
    _, frames, _, antennas = xs[0].shape
    channels, _, beams = real_weight.shape
    group = ROWS // 2
    later = place.shape[0] - 1
    vmem = pl.BlockSpec(memory_space=pltpu.VMEM)
    hbm = pl.BlockSpec(memory_space=pltpu.HBM)
    kept = pltpu.VMEM((later, channels, antennas, beams), real_weight.dtype)
    sums = jax.ShapeDtypeStruct((channels, 2 * subs * pols * frames, beams), jnp.float32)
    return pl.pallas_call(
        functools.partial(first_kernel, subs),
        in_specs=[pl.BlockSpec(memory_space=pltpu.SMEM), vmem, hbm] + [vmem] * (1 + len(xs)),
        out_specs=[vmem] * 2,
        out_shape=[sums, kept],
        scratch_shapes=[
            pltpu.VMEM((channels // group, group, antennas, beams), real_weight.dtype),
            pltpu.SemaphoreType.DMA((channels // group,)),
            pltpu.SemaphoreType.DMA((1, later, LOTS)),
        ],
        compiler_params=pltpu.CompilerParams(vmem_limit_bytes=8 * 2**20),
        cost_estimate=pl.CostEstimate(
            flops=4 * 10**10, bytes_accessed=4 * 10**8, transcendentals=0
        ),
        name="first_beams",
    )(place, sorting(subs, pols, frames), real_weight, imaginary_weight, *xs)


def beam_power(xs, place, kept, imaginary_weight, sums, wides, subs, pols):
    frames = xs[0].shape[1]
    channels, _, beams = sums.shape
    targets = wides * subs
    width = subs * frames * (beams // targets)
    vmem = pl.BlockSpec(memory_space=pltpu.VMEM)
    return pl.pallas_call(
        functools.partial(last_kernel, subs, len(kept)),
        in_specs=[pl.BlockSpec(memory_space=pltpu.SMEM)] + [vmem] * (3 + len(kept) + len(xs)),
        out_specs=vmem,
        out_shape=jax.ShapeDtypeStruct((targets, pols, channels, width), jnp.bfloat16),
        scratch_shapes=[pltpu.VMEM((subs * frames, channels, beams), jnp.float32)],
        compiler_params=pltpu.CompilerParams(vmem_limit_bytes=4 * 2**20),
        name="beam_power",
    )(
        place,
        sorting(subs, pols, frames),
        *(pltpu.with_memory_space_constraint(part, pltpu.VMEM) for part in kept),
        imaginary_weight,
        sums,
        *xs,
    )


def exchange(x, offset, names):
    count = math.prod(lax.axis_size(name) for name in names)
    return lax.ppermute(x, names, [(k, k ^ offset) for k in range(count)])


def dft_table(samples, channels, wides, owners):
    own = channels // owners
    group = ROWS // 2

    def order(part):
        part = part.reshape(wides, owners // wides, own // group, group, 2, samples)
        return part.transpose(0, 1, 2, 4, 3, 5).reshape(wides, -1, samples)

    return np.concatenate([order(part) for part in dft_parts(samples, channels)], axis=1)


def shift_kernel(scale, power_ref, delay_ref, out_ref):
    beams, frames, _ = out_ref.shape
    delays = lax.rem(delay_ref[...], frames)
    power = power_ref[...]
    sums = [None] * frames
    for delay in range(frames):
        chosen = (delays == delay).astype(jnp.float32).astype(jnp.bfloat16)
        picked = lax.dot_general(
            power, chosen, (((0,), (1,)), ((), ())), preferred_element_type=jnp.float32
        )
        for frame in range(frames):
            row = (frame + delay) % frames * beams
            term = picked[row : row + beams]
            sums[frame] = term if sums[frame] is None else sums[frame] + term
    for frame in range(frames):
        out_ref[:, frame, :] = sums[frame] * scale


def shift_and_add(power, delays, frames):
    channels, width = power.shape
    beams = width // frames
    return pl.pallas_call(
        functools.partial(shift_kernel, 1.0 / math.sqrt(channels)),
        out_shape=jax.ShapeDtypeStruct((beams, frames, delays.shape[0]), jnp.float32),
        compiler_params=pltpu.CompilerParams(vmem_limit_bytes=8 * 2**20),
        name="shift_and_add",
    )(power, delays)


def plain_spectra(volts, owners, channels):
    frames, antennas, samples = volts.shape
    upper, lower = (jnp.asarray(part) for part in dft_parts(samples, channels))
    x = sum(
        jnp.einsum("krn,fan->kfra", part, volts, preferred_element_type=jnp.float32)
        for part in (upper, lower)
    )
    x = x.astype(jnp.bfloat16).reshape(owners, channels // owners, frames, 2, antennas)
    return x


def plain_beam_power(x, real_weight, imaginary_weight, wides, subs, pols):
    _, own, frames, _, antennas = x.shape
    beams = real_weight.shape[2]
    x = x.reshape(wides, subs, pols, own, frames, 2, antennas)
    x = x.transpose(3, 5, 2, 1, 4, 0, 6).reshape(own, 2, pols * subs * frames, wides * antennas)
    by_re, by_im = (
        jnp.einsum("crfa,cab->rcfb", x, weight, preferred_element_type=jnp.float32)
        for weight in (real_weight, imaginary_weight)
    )
    power = (by_re[0] - by_im[1]) ** 2 + (by_im[0] + by_re[1]) ** 2
    power = power.reshape(own, pols, subs * frames, beams).sum(axis=1)
    power = power - jnp.mean(power, axis=1, keepdims=True)
    targets = wides * subs
    power = power.reshape(own, subs * frames, targets, beams // targets)
    return power.transpose(2, 0, 1, 3).reshape(targets, own, -1).astype(jnp.bfloat16)


def plain_shift_and_add(power, delays, frames):
    channels = power.shape[0]
    power = power.reshape(channels, frames, -1)
    chosen = (delays[None] % frames == jnp.arange(frames)[:, None, None]).astype(jnp.bfloat16)
    picked = jnp.einsum("dtc,cfb->dbft", chosen, power, preferred_element_type=jnp.float32)
    moved = sum(jnp.roll(picked[delay], -delay, axis=1) for delay in range(frames))
    return moved * (1.0 / math.sqrt(channels))


def local(voltages, real_weight, imaginary_weight, delays):
    highs, lows, subs, pols = (lax.axis_size(name) for name in OWNERS)
    wides = highs * lows
    owners = wides * subs * pols
    own, _, beams = real_weight.shape
    frames = subs * voltages.shape[2]
    tiled = (
        own % ROWS == 0
        and voltages.shape[1] % 128 == 0
        and (beams // (wides * subs)) % 32 == 0
        and frames == 4
        and (wides, subs, pols) == (4, 2, 2)
    )
    turn = functools.partial(
        lax.all_to_all, axis_name=OWNERS, split_axis=0, concat_axis=0, tiled=True
    )
    if not tiled:
        volts = jnp.transpose(voltages[0], (1, 0, 2))
        x = turn(plain_spectra(volts, owners, own * owners))
        power = plain_beam_power(x, real_weight, imaginary_weight, wides, subs, pols)
        power = jnp.broadcast_to(power[:, None], (wides * subs, pols) + power.shape[1:])
        power = turn(power.reshape(owners, own, -1))
        return plain_shift_and_add(power.reshape(owners * own, -1), delays, frames)
    high, low, sub, pol = (lax.axis_index(name) for name in OWNERS)
    side, core = lax.axis_size("wide_low"), sub * pols + pol
    table = jnp.asarray(dft_table(voltages.shape[3], own * owners, wides, owners))
    table = pltpu.with_memory_space_constraint(table, pltpu.HBM)
    real_weight = pltpu.with_memory_space_constraint(real_weight, pltpu.HBM)

    def numbers(*values):
        return jnp.stack(values).astype(jnp.int32)

    wide = high * side + low
    offsets = list(range(side, wides)) + list(range(side))[::-1]
    at = [wide ^ offset for offset in offsets]
    far, (volts,) = spectra(voltages, table, numbers(at[0], core), 1, subs, pols)
    imaginary_weight = imaginary_weight.reshape(own, wides, -1, beams)
    imaginary_weight, _ = lax.optimization_barrier((imaginary_weight, far[0]))
    imaginary_weight = pltpu.with_memory_space_constraint(imaginary_weight, pltpu.VMEM)
    near, near_kept = spectra(
        volts, table, numbers(*at[1:], core), wides - 1, subs, pols, [real_weight], side
    )
    moved = []
    for k, piece in enumerate(far + near):
        offset = (offsets[k // subs] * subs + k % subs) * pols
        moved.append(exchange(piece, offset, OWNERS) if offset else piece)

    def both(pieces, join):
        theirs = [piece[1:] for piece in pieces]
        theirs = [jnp.concatenate(theirs)] if join else theirs
        return [*pieces, *(exchange(part, 1, ("pol",)) for part in theirs)]

    first, _ = lax.optimization_barrier((moved[:subs], near[0]))
    sums, kept = first_beams(
        both(first, False), numbers(*at[:side]), real_weight, imaginary_weight, subs, pols
    )
    rest = moved[subs:]
    longest = rest.pop(2 * subs - 1)
    longest, rest, sums = lax.optimization_barrier((longest, rest, sums))
    rest.insert(2 * subs - 1, longest)
    total = beam_power(
        both(rest, True),
        numbers(sub, *at[1:]),
        [kept] + near_kept,
        imaginary_weight,
        sums,
        wides,
        subs,
        pols,
    )
    power = turn(total.reshape(owners, own, -1))
    return shift_and_add(power.reshape(owners * own, -1), delays, frames)


def solution(mesh):
    names = dict(zip(mesh.axis_names, mesh.devices.shape))
    low = max(1, names["wide"] // 2)
    sizes = (names["group"], names["wide"] // low, low, names["sub"], names["pol"])
    split = jax.sharding.Mesh(mesh.devices.reshape(sizes), ("group",) + OWNERS)
    placed = (
        P("pol", ("group", "wide_high", "wide_low"), "sub", None),
        P(OWNERS, None, None),
        P(OWNERS, None, None),
        P("pol", None),
    )
    return jax.shard_map(
        local,
        mesh=split,
        in_specs=placed,
        out_specs=P(("group", "wide_high", "wide_low", "sub"), None, "pol"),
        check_vma=False,
    )
```
